32 devices in a mesh: sec: 4 (over y, x), fx: 4 (over z), fy: 2 (over core).
Axes of the slice: x: 2, y: 2, z: 4, core: 2. Of those that a mesh axis runs over, the one named last changes fastest.
Arguments:
- conn: int32 [4, 4, 2, 8, 2139], P('sec', 'fx', 'fy'), may hold values from 0 to 3071, as said below
- material: int32 [4, 4, 2, 2139], P('sec', 'fx', 'fy'), may hold values from 0 to 2
- side_nodes: int32 [4, 4, 2, 2, 96], P('sec', 'fx', 'fy'), may hold values from 0 to 3071, as said below
- rim_nodes: int32 [4, 4, 2, 2, 128], P('sec', 'fx', 'fy'), may hold values from 0 to 3071, as said below
- iface_node: int32 [4, 4, 2, 1536], P('sec', 'fx', 'fy'), may hold values from 0 to 3071, as said below
- face_of_row: int32 [4, 4, 3072], P('sec', 'fx'), may hold values from 0 to 3071, each once within a row
- conductivity: float32 [3], replicated, may hold values from 0.5 to 5
- capacity: float32 [3], replicated, may hold values from 0.5 to 2
- diag_part: float32 [4, 4, 2, 3072], P('sec', 'fx', 'fy'), may hold values from 0.2 to 1
- heat_source: float32 [4, 4, 2, 3072], P('sec', 'fx', 'fy'), may hold values from -6 to 6
- air_state: float32 [4, 96, 64, 512], P(None, 'sec', 'fy', 'fx'), may hold values from -6 to 6
Outputs:
- solid_temp: float32 [4, 4, 2, 3072], P('sec', 'fx', 'fy')
- air_next: float32 [4, 96, 64, 512], P(None, 'sec', 'fy', 'fx')
The draws below stay inside these ranges and needn't reach their ends.
Inputs may be any that keep to these rules, and one draw needn't show every extreme that they name: Each tile has a structured grid of 32 x 24 x 4 nodes (width, height, thickness) numbered by its own permutation; column e of conn lists element e's corners, corner 4 a + 2 b + c at thickness offset a, height offset b, width offset c; the columns run in order of corner 0's thickness, then height, then width position. `side_nodes`: row 0 holds the nodes at the lowest width position, row 1 at the highest, both ordered by thickness then height, so that position k of one tile's row 1 is the same physical node as position k of the next tile's row 0. `rim_nodes`: row 0 holds the nodes at the lowest height position, row 1 at the highest, both ordered by thickness then width, matching between tiles in the same way. `iface_node`: distinct nodes within a tile.
All inputs are finite; a program needn't handle non-finite values.
Results may differ from the reference program's by a relative error of at most 0.0001.
Values sent between devices are 32-bit elements; how exact they have to be, the bound alone decides.
No kernel may reach another device: no remote copies, remote signals or barrier semaphores. Data moves between devices by JAX's collectives and lax.ppermute only.
A program may use at most 64 MiB of HBM per device.

```python
import math
import jax
import jax.numpy as jnp
import numpy as np
from jax import lax

NW = 32
NH = 24
NT = 4
MATS = 3
ITERS = 4
CX = 128
CZ = 24
NODES = 3072
ELEMS = 2139
IF_DEV = 1536
AX = 512
AY = 64
AZ = 96
N_SEC = 4
N_FX = 4
N_FY = 2


def tile_numbering(key):
    base = jax.random.fold_in(key, 11)
    keys = jax.random.split(base, N_SEC * N_FX * N_FY)
    perms = jax.vmap(lambda single: jax.random.permutation(single, NW * NH * NT))(keys)
    return perms.reshape(N_SEC, N_FX, N_FY, NW * NH * NT).astype(jnp.int32)


def natural_corners():
    thick_idx, height_idx, width_idx = jnp.meshgrid(jnp.arange(NT - 1), jnp.arange(NH - 1), jnp.arange(NW - 1), indexing='ij')
    corners = []
    for thick_off in (0, 1):
        for height_off in (0, 1):
            for width_off in (0, 1):
                number = ((thick_idx + thick_off) * NH + height_idx + height_off) * NW + width_idx + width_off
                corners.append(number.reshape(-1))
    return jnp.stack(corners).astype(jnp.int32)


def draw_conn(key, part):
    return jnp.take(tile_numbering(key), natural_corners(), axis=-1)


def draw_side_nodes(key, part):
    thick_idx, height_idx = jnp.meshgrid(jnp.arange(NT), jnp.arange(NH), indexing='ij')
    low_side = ((thick_idx * NH + height_idx) * NW).reshape(-1)
    high_side = low_side + NW - 1
    natural = jnp.stack([low_side, high_side]).astype(jnp.int32)
    return jnp.take(tile_numbering(key), natural, axis=-1)


def draw_rim_nodes(key, part):
    thick_idx, width_idx = jnp.meshgrid(jnp.arange(NT), jnp.arange(NW), indexing='ij')
    low_rim = (thick_idx * NH * NW + width_idx).reshape(-1)
    high_rim = low_rim + (NH - 1) * NW
    natural = jnp.stack([low_rim, high_rim]).astype(jnp.int32)
    return jnp.take(tile_numbering(key), natural, axis=-1)


def draw_iface_node(key, part):
    base = jax.random.fold_in(key, 13)
    keys = jax.random.split(base, N_SEC * N_FX * N_FY)
    perms = jax.vmap(lambda single: jax.random.permutation(single, NW * NH * NT)[:IF_DEV])(keys)
    return perms.reshape(N_SEC, N_FX, N_FY, IF_DEV).astype(jnp.int32)


def plant(result, stream_key, least, top_value):
    longest = result.shape.index(max(result.shape))
    spots = []
    for shift in (0, 1):
        where = [jax.random.randint(jax.random.fold_in(stream_key, axis), (), 0, length) for axis, length in enumerate(result.shape)]
        where[longest] = (where[longest] + shift) % result.shape[longest]
        spots.append(tuple(where))
    return result.at[spots[0]].set(least).at[spots[1]].set(top_value)


def steps_of(key, dims, pieces, least, top_value):
    gain, own = 1.0, jax.random.fold_in(key, 6)
    for dim, blocks in pieces:
        steps = jnp.exp(jax.random.uniform(jax.random.fold_in(own, dim), (blocks,), jnp.float32, least / len(pieces), top_value / len(pieces)))
        gain = gain * jnp.repeat(steps, dims[dim] // blocks).reshape([-1 if axis == dim else 1 for axis in range(len(dims))])
    return gain


def normal_values(key, extent, scale, most, pieces=(), dtype=jnp.bfloat16):
    result = scale * jax.random.normal(key, extent, jnp.float32)
    if pieces:
        result = result * steps_of(key, extent, pieces, -0.22, 0.18)
    return jnp.clip(result, -most, most).astype(dtype)


def setup_inputs(seed: int = 0) -> dict:
    streams_of = jax.random.split(jax.random.key(seed), 12)
    conn = draw_conn(jax.random.fold_in(streams_of[11], 71), 0)
    material = plant(jax.random.randint(streams_of[1], (N_SEC, N_FX, N_FY, ELEMS), 0, MATS), jax.random.fold_in(streams_of[1], 1), 0, MATS - 1).astype(jnp.int32)
    side_nodes = draw_side_nodes(jax.random.fold_in(streams_of[11], 71), 0)
    rim_nodes = draw_rim_nodes(jax.random.fold_in(streams_of[11], 71), 0)
    iface_node = draw_iface_node(jax.random.fold_in(streams_of[11], 71), 0)
    face_of_row = jax.vmap(lambda own: jax.random.permutation(own, CZ * CX))(jax.random.split(streams_of[5], N_SEC * N_FX)).reshape((N_SEC, N_FX, CZ * CX)).astype(jnp.int32)
    conductivity = jnp.clip(jnp.exp(jax.random.uniform(streams_of[6], (MATS,), jnp.float32, math.log(0.5), math.log(5.0))), 0.5, 5.0)
    capacity = jnp.clip(jnp.exp(jax.random.uniform(streams_of[7], (MATS,), jnp.float32, math.log(0.5), math.log(2.0))), 0.5, 2.0)
    diag_part = jnp.clip(jnp.exp(math.log(1.0) - 1.609438 * jax.random.uniform(streams_of[8], (N_SEC, N_FX, N_FY, NODES), jnp.float32) ** steps_of(streams_of[8], (N_SEC, N_FX, N_FY, NODES), ((0, 4), (1, 4), (2, 2)), -0.2, 0.2)), 0.2, 1.0)
    heat_source = normal_values(streams_of[9], (N_SEC, N_FX, N_FY, NODES), 1.0, 6.0, ((0, 4), (1, 4), (2, 2)), jnp.float32)
    air_state = normal_values(streams_of[10], (4, AZ, AY, AX), 1.0, 6.0, ((1, 4), (2, 2), (3, 4)), jnp.float32)
    return {"conn": conn, "material": material, "side_nodes": side_nodes, "rim_nodes": rim_nodes, "iface_node": iface_node, "face_of_row": face_of_row, "conductivity": conductivity, "capacity": capacity, "diag_part": diag_part, "heat_source": heat_source, "air_state": air_state}


time_step = 0.2
viscosity = 0.75


def unit_stiffness():
    table = np.zeros((8, 8), np.float32)
    for row_id in range(8):
        for col_id in range(8):
            differ = row_id ^ col_id
            bits = (differ & 1) + ((differ >> 1) & 1) + ((differ >> 2) & 1)
            if bits == 0:
                table[row_id, col_id] = 1.0 / 3.0
            elif bits == 1:
                table[row_id, col_id] = 0.0
            else:
                table[row_id, col_id] = -1.0 / 12.0
    return table


def to_tiles(array):
    moved = jnp.moveaxis(array, 1, 0)
    return moved.reshape((N_FX, N_SEC * N_FY) + moved.shape[3:])


def from_tiles(array):
    shaped = array.reshape((N_FX, N_SEC, N_FY) + array.shape[2:])
    return jnp.moveaxis(shaped, 0, 1)


def scatter_add(values, indices, extra):
    return values.at[indices].add(extra)


def pick_rows(values, indices):
    return values[indices]


def assemble(field, sides, rims):
    adder = jax.vmap(jax.vmap(scatter_add))
    picker = jax.vmap(jax.vmap(pick_rows))
    low_edge = picker(field, sides[:, :, 0])
    high_edge = picker(field, sides[:, :, 1])
    from_prev = jnp.concatenate([jnp.zeros_like(high_edge[:1]), high_edge[:-1]], 0)
    from_next = jnp.concatenate([low_edge[1:], jnp.zeros_like(low_edge[:1])], 0)
    field = adder(field, sides[:, :, 0], from_prev)
    field = adder(field, sides[:, :, 1], from_next)
    low_edge = picker(field, rims[:, :, 0])
    high_edge = picker(field, rims[:, :, 1])
    from_prev = jnp.concatenate([jnp.zeros_like(high_edge[:, :1]), high_edge[:, :-1]], 1)
    from_next = jnp.concatenate([low_edge[:, 1:], jnp.zeros_like(low_edge[:, :1])], 1)
    field = adder(field, rims[:, :, 0], from_prev)
    field = adder(field, rims[:, :, 1], from_next)
    return field


def apply_tile(direction, links, kinds, conductivity, capacity):
    stiffness = jnp.asarray(unit_stiffness(), jnp.float32)
    element_vals = jnp.take(direction, links, axis=0)
    conduct = conductivity[kinds]
    storage = 0.125 * capacity[kinds]
    flux = jnp.dot(stiffness, element_vals, precision=lax.Precision.HIGHEST)
    element_out = conduct * flux + storage * element_vals
    return jnp.zeros(direction.shape, jnp.float32).at[links.reshape(-1)].add(element_out.reshape(-1))


def advance(padded):
    centre = padded[:, 1:-1, 1:-1, 1:-1]
    vel_x = centre[1]
    vel_y = centre[2]
    vel_z = centre[3]
    fields = []
    for field_id in range(4):
        layer = padded[field_id]
        middle = centre[field_id]
        east = layer[1:-1, 1:-1, 2:]
        west = layer[1:-1, 1:-1, :-2]
        north = layer[1:-1, 2:, 1:-1]
        south = layer[1:-1, :-2, 1:-1]
        upper = layer[2:, 1:-1, 1:-1]
        lower = layer[:-2, 1:-1, 1:-1]
        transport = vel_x * (east - west) * 0.5 + vel_y * (north - south) * 0.5 + vel_z * (upper - lower) * 0.5
        spread = east + west + north + south + upper + lower - 6.0 * middle
        fields.append(middle - time_step * transport + time_step * viscosity * spread)
    return jnp.stack(fields)


def reference(conn, material, side_nodes, rim_nodes, iface_node, face_of_row, conductivity, capacity, diag_part, heat_source, air_state):
    links = to_tiles(conn)
    kinds = to_tiles(material)
    sides = to_tiles(side_nodes)
    rims = to_tiles(rim_nodes)

    def operate(direction):
        local = jax.vmap(jax.vmap(lambda field, link_tab, kind_tab: apply_tile(field, link_tab, kind_tab, conductivity, capacity)))(direction, links, kinds)
        return assemble(local, sides, rims)

    mult = assemble(jnp.ones(to_tiles(diag_part).shape, jnp.float32), sides, rims)
    diagonal = assemble(to_tiles(diag_part), sides, rims)
    rhs = assemble(to_tiles(heat_source), sides, rims)
    weight = 1.0 / mult

    def inner(left_vec, right_vec):
        return jnp.sum(weight * left_vec * right_vec)

    solution = jnp.zeros_like(rhs)
    residual = rhs
    scaled = residual / diagonal
    direction = scaled
    gamma = inner(residual, scaled)
    for iteration in range(ITERS):
        image = operate(direction)
        step_len = gamma / inner(direction, image)
        solution = solution + step_len * direction
        residual = residual - step_len * image
        if iteration + 1 < ITERS:
            scaled = residual / diagonal
            gamma_next = inner(residual, scaled)
            direction = scaled + (gamma_next / gamma) * direction
            gamma = gamma_next
    solid_temp = from_tiles(solution)

    values = jnp.take_along_axis(solid_temp, iface_node, axis=-1)
    values = values.reshape(N_SEC, N_FX, N_FY * values.shape[-1])
    faces = jax.vmap(jax.vmap(lambda indices, extra: jnp.zeros((CZ * CX,), jnp.float32).at[indices].set(extra)))(face_of_row, values)
    wall = faces.reshape(N_SEC, N_FX, CZ, CX).transpose(0, 2, 1, 3).reshape(N_SEC * CZ, N_FX * CX)

    padded = jnp.pad(air_state, ((0, 0), (1, 1), (1, 1), (1, 1)))
    padded = padded.at[0, 1:-1, 0, 1:-1].set(wall)
    air_next = advance(padded)
    return solid_temp, air_next
```

```python
import jax
import jax.numpy as jnp
import numpy as np
from jax import lax
from jax.experimental import pallas as pl
from jax.experimental.pallas import tpu as pltpu
from jax.sharding import PartitionSpec as P

NW = 32
NH = 24
NT = 4
ITERS = 4
LANES = 128
SUBS = 8

time_step = 0.2
viscosity = 0.75

VMEM = pl.BlockSpec(memory_space=pltpu.VMEM)
SMEM = pl.BlockSpec(memory_space=pltpu.SMEM)
ANY = pl.BlockSpec(memory_space=pl.ANY)
PARAMS = pltpu.CompilerParams(vmem_limit_bytes=56 * 1024 * 1024)

EW = NW - 1
EH = NH - 1
ET = NT - 1
ELEMS = ET * EH * EW
ROWS = NT * NH * NW // LANES
FIELD_ROWS = NT * NH
BAND_ROWS = 2 * FIELD_ROWS + ET * NH


def iota(shape, dim):
    return lax.broadcasted_iota(jnp.int32, shape, dim)


def lane_pick(row, idx):
    return jnp.take_along_axis(
        jnp.broadcast_to(row, idx.shape), idx, axis=1, mode="promise_in_bounds"
    )


def look_up(rows, place):
    high = place >> 7
    low = place & (LANES - 1)
    out = None
    for r, row in enumerate(rows):
        got = lane_pick(row, low)
        out = got if out is None else jnp.where(high == r, got, out)
    return out


def spread(idx, values):
    count = idx.shape[0]
    acc = None
    group = 4
    for start in range(0, count, group):
        left, right = [], []
        for r in range(start, start + group):
            row = idx[r : r + 1]
            hot_high = iota((count, LANES), 0) == (row >> 7)
            hot_low = iota((LANES, LANES), 0) == (row & (LANES - 1))
            left.append(
                jnp.concatenate(
                    [jnp.where(hot_high, v[r : r + 1], 0.0) for v in values], axis=0
                ).astype(jnp.bfloat16)
            )
            right.append(jnp.where(hot_low, 1.0, 0.0).astype(jnp.bfloat16))
        part = lax.dot_general(
            jnp.concatenate(left, axis=1),
            jnp.concatenate(right, axis=1),
            (((1,), (1,)), ((), ())),
            preferred_element_type=jnp.float32,
        )
        acc = part if acc is None else acc + part
    return [acc[i * count : (i + 1) * count] for i in range(len(values))]


def element_keys():
    h = np.arange(NH)[:, None]
    lane = np.arange(LANES)[None, :]
    t, w = lane // NW, lane % NW
    corner = 4 * (t == NT - 1) + 2 * (h == NH - 1) + (w == NW - 1)
    column = np.minimum(t, ET - 1) * EH * EW + np.minimum(h, EH - 1) * EW + np.minimum(w, EW - 1)
    return corner, column


def stage_kernel(conn_ref, material_ref, diag_ref, source_ref, pay_ref, nodes_ref):
    corner_np, column_np = element_keys()
    pieces, kinds = [], []
    for j in range(NH // SUBS):
        h = iota((SUBS, LANES), 0) + SUBS * j
        lane = iota((SUBS, LANES), 1)
        t = lane >> 5
        w = lane & (NW - 1)
        corner = (
            jnp.where(t == NT - 1, 4, 0) + jnp.where(h == NH - 1, 2, 0) + jnp.where(w == NW - 1, 1, 0)
        )
        column = (
            jnp.minimum(t, ET - 1) * (EH * EW)
            + jnp.minimum(h, EH - 1) * EW
            + jnp.minimum(w, EW - 1)
        )
        low = column & (LANES - 1)
        tile = column >> 7
        key = tile * 8 + corner
        rows = slice(SUBS * j, SUBS * (j + 1))
        wanted = sorted(set((column_np[rows] // LANES * 8 + corner_np[rows]).reshape(-1).tolist()))
        out = jnp.zeros((SUBS, LANES), jnp.int32)
        for code in wanted:
            c, k = code % 8, code // 8
            row = conn_ref[c : c + 1, LANES * k : LANES * (k + 1)]
            out = jnp.where(key == code, lane_pick(row, low), out)
        pieces.append(out)
        kind = jnp.full((SUBS, LANES), -1, jnp.int32)
        for k in sorted({code // 8 for code in wanted if code % 8 == 0}):
            row = material_ref[0:1, LANES * k : LANES * (k + 1)]
            kind = jnp.where((corner == 0) & (tile == k), lane_pick(row, low), kind)
        kinds.append(kind)
    nodes = jnp.concatenate(pieces, axis=0)
    nodes_ref[...] = nodes
    pay_ref[0:ROWS] = look_up([diag_ref[r : r + 1] for r in range(ROWS)], nodes)
    pay_ref[ROWS : 2 * ROWS] = look_up([source_ref[r : r + 1] for r in range(ROWS)], nodes)
    pay_ref[2 * ROWS : 3 * ROWS] = jnp.concatenate(kinds, axis=0).astype(jnp.float32) + 1.0


def band_kernel(tiles_x, wide, where_ref, *refs):
    parts, band_ref, held = refs[:tiles_x], refs[tiles_x], refs[tiles_x + 1]
    fx = where_ref[1]
    for k, part in enumerate(parts):
        held[fx ^ k] = part[...]
    lane = iota((NH, wide), 1)
    at = 0
    for field in range(3):
        for t in range(NT if field < 2 else ET):
            total = None
            for f in range(tiles_x):
                x = held[f, field * ROWS : (field + 1) * ROWS]
                if wide > LANES:
                    x = jnp.concatenate([x, jnp.zeros((NH, wide - LANES), jnp.float32)], axis=1)
                shift = (EW * f - NW * t) % wide
                if shift:
                    x = pltpu.roll(x, shift, 1)
                x = jnp.where((lane >= EW * f) & (lane < EW * f + NW), x, 0.0)
                total = x if total is None else total + x
            band_ref[at : at + NH] = total
            at += NH


def faces_kernel(where_ref, air_ref, x_even, x_odd, y_even, y_odd, z_even, z_odd):
    sec, fx, fy = where_ref[0], where_ref[1], where_ref[2]
    fields, cells_z, cells_y, cells_x = air_ref.shape
    z_up = (sec & 1) == 0
    z_even[...] = air_ref[:, jnp.where(z_up, cells_z - 1, 0)]
    z_odd[...] = air_ref[:, jnp.where(z_up, 0, cells_z - 1)]
    y_up = (fy & 1) == 0
    x_up = (fx & 1) == 0
    lane = iota((cells_y, LANES), 1)
    lows, highs = [], []
    for f in range(fields):
        first = air_ref[f, :, 0, :]
        last = air_ref[f, :, cells_y - 1, :]
        y_even[f] = jnp.where(y_up, last, first)
        y_odd[f] = jnp.where(y_up, first, last)
        low = jnp.zeros((cells_y, LANES), jnp.float32)
        high = jnp.zeros((cells_y, LANES), jnp.float32)
        for z in range(cells_z):
            x = pltpu.roll(air_ref[f, z], z + 1, 1)
            high = jnp.where(lane == z, x, high)
            low = jnp.where(lane == z + 1, x, low)
        lows.append(low)
        highs.append(high)
    low = pltpu.roll(jnp.concatenate(lows, axis=0), LANES - 1, 1)
    high = jnp.concatenate(highs, axis=0)
    x_even[...] = jnp.where(x_up, high, low).T[:cells_z]
    x_odd[...] = jnp.where(x_up, low, high).T[:cells_z]


def air_kernel(
    where_ref, air_ref, x_even, x_odd, y_even, y_odd, z_even, z_odd, next_ref, edge_ref, gain_ref,
    west_ref, east_ref,
):
    sec, fx, fy = where_ref[0], where_ref[1], where_ref[2]
    fields, cells_z, cells_y, cells_x = air_ref.shape
    pad = jnp.zeros((LANES - cells_z, LANES), jnp.float32)
    even = jnp.concatenate([x_even[...], pad], axis=0).T
    odd = jnp.concatenate([x_odd[...], pad], axis=0).T
    x_up = (fx & 1) == 0
    west_ref[...] = jnp.where(x_up, odd, even)
    east_ref[...] = jnp.where(x_up, even, odd)
    y_up = (fy & 1) == 0
    z_up = (sec & 1) == 0
    row = iota((cells_y, LANES), 0)
    lane = iota((cells_y, LANES), 1)
    half = 0.5 * time_step
    mix = time_step * viscosity

    def layer(z, below, above):
        u, v, w = air_ref[1, z], air_ref[2, z], air_ref[3, z]
        hu, hv, hw = half * u, half * v, half * w
        gain_ref[pl.ds(z, 1), :] = (mix + hv[0:1]) * jnp.where(fy == 0, 1.0, 0.0)
        for f in range(fields):
            x = air_ref[f, z]
            span = slice(f * cells_y, (f + 1) * cells_y)
            west = jnp.where(
                lane == 0,
                pltpu.roll(west_ref[span], (LANES - z) % LANES, 1),
                pltpu.roll(x, 1, 1),
            )
            east = jnp.where(
                lane == LANES - 1,
                pltpu.roll(east_ref[span], LANES - 1 - z, 1),
                pltpu.roll(x, LANES - 1, 1),
            )
            y_e, y_o = y_even[f, pl.ds(z, 1), :], y_odd[f, pl.ds(z, 1), :]
            south_ghost = jnp.where(y_up, y_o, y_e)
            north_ghost = jnp.where(y_up, y_e, y_o)
            south = jnp.where(row == 0, south_ghost, pltpu.roll(x, 1, 0))
            north = jnp.where(row == cells_y - 1, north_ghost, pltpu.roll(x, cells_y - 1, 0))
            lower, upper = below(f), above(f)
            out = (
                (1.0 - 6.0 * mix) * x
                + mix * (east + west + north + south + upper + lower)
                + hu * (west - east)
                + hv * (south - north)
                + hw * (lower - upper)
            )
            next_ref[f, z] = out
            if f == 0:
                edge_ref[z] = out[:SUBS]

    def ghost_low(f):
        return jnp.where(z_up, z_odd[f], z_even[f])

    def ghost_high(f):
        return jnp.where(z_up, z_even[f], z_odd[f])

    layer(0, ghost_low, lambda f: air_ref[f, 1])

    @pl.loop(1, cells_z - 1)
    def _(z):
        layer(z, lambda f: air_ref[f, z - 1], lambda f: air_ref[f, z + 1])

    layer(cells_z - 1, lambda f: air_ref[f, cells_z - 2], ghost_high)


def place_kernel(nodes_ref, iface_ref, place_ref, rows_ref):
    nodes = nodes_ref[...]
    at_row = iota(nodes.shape, 0).astype(jnp.float32)
    at_lane = iota(nodes.shape, 1).astype(jnp.float32)
    high, low = spread(nodes, [at_row, at_lane])
    place = high * LANES + low
    place_ref[...] = place.astype(jnp.int32)
    rows_ref[...] = look_up([place[r : r + 1] for r in range(ROWS)], iface_ref[...])


def face_kernel(tiles_y, where_ref, face_ref, *refs):
    parts, wall_ref, held = refs[:tiles_y], refs[tiles_y], refs[tiles_y + 1]
    fy = where_ref[2]
    for k, part in enumerate(parts):
        held[fy ^ k] = part[...] + (fy ^ k).astype(jnp.float32) * (ROWS * LANES)
    rows = jnp.concatenate([held[j] for j in range(tiles_y)], axis=0)
    row = rows.astype(jnp.int32)
    high, low = spread(
        face_ref[...],
        [(row >> 7).astype(jnp.float32), (row & (LANES - 1)).astype(jnp.float32)],
    )
    wall_ref[...] = (high * LANES + low).astype(jnp.int32)


def solve_kernel(
    tiles_s, tiles_x, tiles_y, wide, material_count,
    where_ref, conduct_ref, capacity_ref, place_ref, wall_ref, edge_ref, gain_ref, air_ref, *refs,
):
    bands = tiles_s * tiles_y
    parts = refs[:bands]
    solid_ref, next_ref = refs[bands : bands + 2]
    (held, elem, side, main, inv, res, dirn, image, sol, table, edge, sem) = refs[bands + 2 :]
    sec, fx, fy = where_ref[0], where_ref[1], where_ref[2]
    for j in range(tiles_y):
        for k in range(tiles_s):
            held[(sec ^ k) * tiles_y + (fy ^ j)] = parts[j * tiles_s + k][...]

    lane = iota((NH, wide), 1)
    first_row = iota((NH, wide), 0) == 0
    used = lane < EW * tiles_x + 1

    def right(x):
        return pltpu.roll(x, wide - 1, 1)

    def left(x):
        return pltpu.roll(x, 1, 1)

    def up(x):
        return pltpu.roll(x, NH - 1, 0)

    def down(x):
        return pltpu.roll(x, 1, 0)

    def to_nodes(x):
        x = x + left(x)
        return x + down(x)

    def seams(ref):
        for k in range(1, bands):
            for t in range(NT):
                both = ref[k - 1, t, NH - 1 : NH, :] + ref[k, t, 0:1, :]
                ref[k - 1, t, NH - 1 : NH, :] = both
                ref[k, t, 0:1, :] = both

    def each_band(body, total=None):
        return lax.fori_loop(0, bands, body, total)

    def prepare(b, _):
        cells, own = [], []
        for t in range(ET):
            kind = held[b, 2 * FIELD_ROWS + t * NH : 2 * FIELD_ROWS + (t + 1) * NH, :]
            x = jnp.zeros_like(kind)
            s = jnp.zeros_like(kind)
            for m in range(material_count):
                x = jnp.where(kind == m + 1.0, conduct_ref[m] * (1.0 / 12.0), x)
                s = jnp.where(kind == m + 1.0, capacity_ref[m] * 0.125, s)
            elem[b, t] = x
            side[b, t] = to_nodes(x)
            cells.append(x)
            own.append(5.0 * x + s)
        for t in range(NT):
            if t == 0:
                m = own[0]
            elif t == NT - 1:
                m = own[ET - 1]
            else:
                m = own[t] + own[t - 1]
            main[b, t] = to_nodes(m)
            inv[b, t] = held[b, t * NH : (t + 1) * NH, :]
            res[b, t] = held[b, FIELD_ROWS + t * NH : FIELD_ROWS + (t + 1) * NH, :]
        return _

    each_band(prepare)
    seams(inv)
    seams(res)

    zero = jnp.zeros((NH, wide), jnp.float32)

    def count_once(b, x):
        return jnp.where(first_row & (b > 0), 0.0, x)

    def total_of(x):
        return jnp.sum(jnp.sum(x, axis=0, keepdims=True), axis=1, keepdims=True)

    def begin(b, acc):
        for t in range(NT):
            d = jnp.where(used, 1.0 / inv[b, t], 0.0)
            inv[b, t] = d
            r = res[b, t]
            z = r * d
            dirn[b, t] = z
            sol[b, t] = zero
            acc = acc + count_once(b, r * z)
        return acc

    gamma = total_of(each_band(begin, zero))

    beta = None
    for iteration in range(ITERS):

        def operate(b, acc, beta=beta):
            p, cross, diag, layer = [], [], [], []
            for t in range(NT):
                x = dirn[b, t]
                if beta is not None:
                    x = res[b, t] * inv[b, t] + beta * x
                    dirn[b, t] = x
                y = right(x)
                d = x + up(y)
                c = y + up(x)
                p.append(x)
                diag.append(d)
                cross.append(c)
                layer.append(d + c)
            for t in range(NT):
                out = main[b, t] * p[t]
                if t == 0:
                    both = elem[b, 0]
                    other = both * layer[1]
                    out = out + side[b, 0] * p[1]
                elif t == NT - 1:
                    both = elem[b, ET - 1]
                    other = both * layer[ET - 1]
                    out = out + side[b, ET - 1] * p[ET - 1]
                else:
                    both = elem[b, t] + elem[b, t - 1]
                    other = elem[b, t] * layer[t + 1] + elem[b, t - 1] * layer[t - 1]
                    out = out + side[b, t] * p[t + 1] + side[b, t - 1] * p[t - 1]
                on_diag = other + both * diag[t]
                on_cross = other + both * cross[t]
                out = out - (on_diag + left(on_cross)) - down(on_cross + left(on_diag))
                image[b, t] = out
                acc = acc + p[t] * out
            return acc

        step_len = gamma / total_of(each_band(operate, zero))
        last = iteration + 1 == ITERS
        if not last:
            seams(image)

        def update(b, acc, step_len=step_len, last=last):
            for t in range(NT):
                sol[b, t] = sol[b, t] + step_len * dirn[b, t]
                if not last:
                    r = res[b, t] - step_len * image[b, t]
                    res[b, t] = r
                    acc = acc + count_once(b, r * r * inv[b, t])
            return acc

        gamma_next = total_of(each_band(update, zero))
        if not last:
            beta = gamma_next / gamma
            gamma = gamma_next

    for j in range(tiles_y):
        packed = jnp.zeros((NH, LANES), jnp.float32)
        spot = iota((NH, LANES), 1) >> 5
        for t in range(NT):
            x = sol[sec * tiles_y + j, t]
            x = pltpu.roll(x, (NW * t - EW * fx + tiles_x * wide) % wide, 1)[:, :LANES]
            packed = jnp.where(spot == t, x, packed)
        table[j] = packed
    solid_ref[...] = look_up([table[fy, r : r + 1] for r in range(ROWS)], place_ref[...])
    rows = [table[j, r : r + 1] for j in range(tiles_y) for r in range(ROWS)]
    extra = look_up(rows, wall_ref[...]) * gain_ref[...]
    cells_z = edge_ref.shape[0]
    top = iota((SUBS, LANES), 0) == 0
    for z in range(cells_z):
        edge[z] = edge_ref[z] + jnp.where(top, extra[z : z + 1], 0.0)
    copy = pltpu.make_async_copy(edge, next_ref.at[0, :, 0:SUBS, :], sem)
    copy.start()
    copy.wait()


def swap(x, axis, mask):
    count = lax.axis_size(axis)
    return lax.ppermute(x, axis, [(i, i ^ mask) for i in range(count)])


def pair_swap(x, axis, odd):
    count = lax.axis_size(axis)
    pairs = []
    for i in range(odd, count - 1, 2):
        pairs += [(i, i + 1), (i + 1, i)]
    return lax.ppermute(x, axis, pairs) if pairs else jnp.zeros_like(x)


def on_device(
    conn,
    material,
    side_nodes,
    rim_nodes,
    iface_node,
    face_of_row,
    conductivity,
    capacity,
    diag_part,
    heat_source,
    air_state,
):
    f32 = jnp.float32
    tiles_s, tiles_x, tiles_y = (lax.axis_size(axis) for axis in ("sec", "fx", "fy"))
    bands = tiles_s * tiles_y
    wide = -(-(EW * tiles_x + 1) // LANES) * LANES
    elem_lanes = -(-ELEMS // LANES) * LANES
    where = jnp.stack([lax.axis_index(axis) for axis in ("sec", "fx", "fy")]).astype(jnp.int32)
    fields, cells_z, cells_y, cells_x = air_state.shape

    def shape(*dims):
        return jax.ShapeDtypeStruct(dims, f32)

    def whole(*dims):
        return pl.BlockSpec(dims, lambda i: (0,) * len(dims))

    pay, nodes = pl.pallas_call(
        stage_kernel,
        grid=(1,),
        in_specs=[whole(8, elem_lanes), whole(1, elem_lanes), whole(ROWS, LANES), whole(ROWS, LANES)],
        out_specs=[whole(3 * ROWS, LANES), whole(ROWS, LANES)],
        out_shape=[shape(3 * ROWS, LANES), jax.ShapeDtypeStruct((ROWS, LANES), jnp.int32)],
        compiler_params=PARAMS,
    )(
        conn.reshape(conn.shape[-2:]),
        material.reshape(1, -1),
        diag_part.reshape(ROWS, LANES),
        heat_source.reshape(ROWS, LANES),
    )
    pays = [pay] + [swap(pay, "fx", k) for k in range(1, tiles_x)]

    faces = pl.pallas_call(
        faces_kernel,
        in_specs=[SMEM, VMEM],
        out_specs=[VMEM] * 6,
        out_shape=[shape(cells_z, fields * cells_y)] * 2
        + [shape(fields, cells_z, cells_x)] * 2
        + [shape(fields, cells_y, cells_x)] * 2,
        compiler_params=PARAMS,
    )(where, air_state)
    x_even, x_odd, y_even, y_odd, z_even, z_odd = faces

    band = pl.pallas_call(
        lambda *refs: band_kernel(tiles_x, wide, *refs),
        in_specs=[SMEM] + [VMEM] * tiles_x,
        out_specs=VMEM,
        out_shape=shape(BAND_ROWS, wide),
        scratch_shapes=[pltpu.VMEM((tiles_x, 3 * ROWS, LANES), f32)],
        compiler_params=PARAMS,
    )(where, *pays)

    own_bands = [band] + [swap(band, "sec", k) for k in range(1, tiles_s)]
    all_bands = own_bands + [swap(b, "fy", j) for j in range(1, tiles_y) for b in own_bands]

    place, rows = pl.pallas_call(
        place_kernel,
        in_specs=[VMEM] * 2,
        out_specs=[VMEM] * 2,
        out_shape=[
            jax.ShapeDtypeStruct((ROWS, LANES), jnp.int32),
            shape(iface_node.shape[-1] // LANES, LANES),
        ],
        compiler_params=PARAMS,
    )(nodes, iface_node.reshape(-1, LANES))
    all_rows = [rows] + [swap(rows, "fy", j) for j in range(1, tiles_y)]
    wall = pl.pallas_call(
        lambda *refs: face_kernel(tiles_y, *refs),
        in_specs=[SMEM, VMEM] + [VMEM] * tiles_y,
        out_specs=VMEM,
        out_shape=jax.ShapeDtypeStruct((cells_z, LANES), jnp.int32),
        scratch_shapes=[pltpu.VMEM((tiles_y,) + rows.shape, f32)],
        compiler_params=PARAMS,
    )(where, face_of_row.reshape(-1, LANES), *all_rows)

    ghosts = [
        pair_swap(x_even, "fx", 0),
        pair_swap(x_odd, "fx", 1),
        pair_swap(y_even, "fy", 0),
        pair_swap(y_odd, "fy", 1),
        pair_swap(z_even, "sec", 0),
        pair_swap(z_odd, "sec", 1),
    ]
    air_next, edge, gain = pl.pallas_call(
        air_kernel,
        in_specs=[SMEM] + [VMEM] * 7,
        out_specs=[VMEM] * 3,
        out_shape=[shape(*air_state.shape), shape(cells_z, SUBS, LANES), shape(cells_z, LANES)],
        scratch_shapes=[pltpu.VMEM((LANES, LANES), f32)] * 2,
        compiler_params=PARAMS,
    )(where, air_state, *ghosts)

    grid = (bands, NT, NH, wide)
    solid, air_next = pl.pallas_call(
        lambda *refs: solve_kernel(
            tiles_s, tiles_x, tiles_y, wide, conductivity.shape[0], *refs
        ),
        in_specs=[SMEM] * 3 + [VMEM] * 4 + [ANY] + [VMEM] * bands,
        out_specs=[VMEM, ANY],
        out_shape=[shape(ROWS, LANES), shape(*air_state.shape)],
        input_output_aliases={7: 1},
        scratch_shapes=[pltpu.VMEM((bands, BAND_ROWS, wide), f32)]
        + [pltpu.VMEM((bands, ET, NH, wide), f32)] * 2
        + [pltpu.VMEM(grid, f32)] * 6
        + [
            pltpu.VMEM((tiles_y, ROWS, LANES), f32),
            pltpu.VMEM((cells_z, SUBS, LANES), f32),
            pltpu.SemaphoreType.DMA,
        ],
        compiler_params=PARAMS,
    )(where, conductivity, capacity, place, wall, edge, gain, air_next, *all_bands)
    return solid.reshape(diag_part.shape), air_next


def solution(mesh):
    return jax.shard_map(
        on_device,
        mesh=mesh,
        in_specs=(
            P("sec", "fx", "fy", None, None),
            P("sec", "fx", "fy", None),
            P("sec", "fx", "fy", None, None),
            P("sec", "fx", "fy", None, None),
            P("sec", "fx", "fy", None),
            P("sec", "fx", None),
            P(),
            P(),
            P("sec", "fx", "fy", None),
            P("sec", "fx", "fy", None),
            P(None, "sec", "fy", "fx"),
        ),
        out_specs=(P("sec", "fx", "fy", None), P(None, "sec", "fy", "fx")),
        check_vma=False,
    )
```

```python
import jax
import jax.numpy as jnp
import numpy as np
from jax import lax
from jax.experimental import pallas as pl
from jax.experimental.pallas import tpu as pltpu
from jax.sharding import PartitionSpec as P

NW = 32
NH = 24
NT = 4
ITERS = 4
LANES = 128
SUBS = 8

time_step = 0.2
viscosity = 0.75

VMEM = pl.BlockSpec(memory_space=pltpu.VMEM)
SMEM = pl.BlockSpec(memory_space=pltpu.SMEM)
ANY = pl.BlockSpec(memory_space=pl.ANY)

EW = NW - 1
EH = NH - 1
ET = NT - 1
ELEMS = ET * EH * EW
ROWS = NT * NH * NW // LANES
FIELD_ROWS = NT * NH
BAND_ROWS = 2 * FIELD_ROWS + ET * NH


def iota(shape, dim):
    return lax.broadcasted_iota(jnp.int32, shape, dim)


def lane_pick(row, idx):
    return jnp.take_along_axis(
        jnp.broadcast_to(row, idx.shape), idx, axis=1, mode="promise_in_bounds"
    )


def look_up(rows, place):
    high = place >> 7
    low = place & (LANES - 1)
    out = None
    for r, row in enumerate(rows):
        got = lane_pick(row, low)
        out = got if out is None else jnp.where(high == r, got, out)
    return out


def spread(idx, values):
    count = idx.shape[0]
    acc = None
    group = 4
    for start in range(0, count, group):
        left, right = [], []
        for r in range(start, start + group):
            row = idx[r : r + 1]
            hot_high = iota((count, LANES), 0) == (row >> 7)
            hot_low = iota((LANES, LANES), 0) == (row & (LANES - 1))
            left.append(
                jnp.concatenate(
                    [jnp.where(hot_high, v[r : r + 1], 0.0) for v in values], axis=0
                ).astype(jnp.bfloat16)
            )
            right.append(jnp.where(hot_low, 1.0, 0.0).astype(jnp.bfloat16))
        part = lax.dot_general(
            jnp.concatenate(left, axis=1),
            jnp.concatenate(right, axis=1),
            (((1,), (1,)), ((), ())),
            preferred_element_type=jnp.float32,
        )
        acc = part if acc is None else acc + part
    return [acc[i * count : (i + 1) * count] for i in range(len(values))]


def element_keys():
    h = np.arange(NH)[:, None]
    lane = np.arange(LANES)[None, :]
    t, w = lane // NW, lane % NW
    corner = 4 * (t == NT - 1) + 2 * (h == NH - 1) + (w == NW - 1)
    column = np.minimum(t, ET - 1) * EH * EW + np.minimum(h, EH - 1) * EW + np.minimum(w, EW - 1)
    return corner, column


def stage_kernel(
    conn_ref, material_ref, diag_ref, source_ref, air_hbm,
    plain_ref, even_ref, odd_ref, nodes_ref, y_even, y_odd, z_even, z_odd, air_ref,
    sem,
):
    sec, fx, fy = (lax.axis_index(axis) for axis in ("sec", "fx", "fy"))
    load = pltpu.make_async_copy(air_hbm, air_ref, sem)
    load.start()
    corner_np, column_np = element_keys()
    pieces, kinds = [], []
    for j in range(NH // SUBS):
        h = iota((SUBS, LANES), 0) + SUBS * j
        lane = iota((SUBS, LANES), 1)
        t = lane >> 5
        w = lane & (NW - 1)
        corner = (
            jnp.where(t == NT - 1, 4, 0) + jnp.where(h == NH - 1, 2, 0) + jnp.where(w == NW - 1, 1, 0)
        )
        column = (
            jnp.minimum(t, ET - 1) * (EH * EW)
            + jnp.minimum(h, EH - 1) * EW
            + jnp.minimum(w, EW - 1)
        )
        low = column & (LANES - 1)
        tile = column >> 7
        key = tile * 8 + corner
        rows = slice(SUBS * j, SUBS * (j + 1))
        wanted = sorted(set((column_np[rows] // LANES * 8 + corner_np[rows]).reshape(-1).tolist()))
        out = jnp.zeros((SUBS, LANES), jnp.int32)
        for code in wanted:
            c, k = code % 8, code // 8
            row = conn_ref[c : c + 1, LANES * k : LANES * (k + 1)]
            out = jnp.where(key == code, lane_pick(row, low), out)
        pieces.append(out)
        kind = jnp.full((SUBS, LANES), -1, jnp.int32)
        for k in sorted({code // 8 for code in wanted if code % 8 == 0}):
            row = material_ref[0:1, LANES * k : LANES * (k + 1)]
            kind = jnp.where((corner == 0) & (tile == k), lane_pick(row, low), kind)
        kinds.append(kind)
    nodes = jnp.concatenate(pieces, axis=0)
    nodes_ref[...] = nodes
    diag = look_up([diag_ref[r : r + 1] for r in range(ROWS)], nodes)
    source = look_up([source_ref[r : r + 1] for r in range(ROWS)], nodes)
    kind = jnp.concatenate(kinds, axis=0).astype(jnp.float32) + 1.0
    for ref in (plain_ref, even_ref, odd_ref):
        ref[0:ROWS] = diag
        ref[ROWS : 2 * ROWS] = source
        ref[2 * ROWS : 3 * ROWS] = kind

    load.wait()
    fields, cells_z, cells_y, cells_x = air_ref.shape
    z_up = (sec & 1) == 0
    z_even[...] = air_ref[:, jnp.where(z_up, cells_z - 1, 0)]
    z_odd[...] = air_ref[:, jnp.where(z_up, 0, cells_z - 1)]
    y_up = (fy & 1) == 0
    x_up = (fx & 1) == 0
    lane = iota((cells_y, LANES), 1)
    lows, highs = [], []
    for f in range(fields):
        first = air_ref[f, :, 0, :]
        last = air_ref[f, :, cells_y - 1, :]
        y_even[f] = jnp.where(y_up, last, first)
        y_odd[f] = jnp.where(y_up, first, last)
        low = jnp.zeros((cells_y, LANES), jnp.float32)
        high = jnp.zeros((cells_y, LANES), jnp.float32)
        for z in range(cells_z):
            x = pltpu.roll(air_ref[f, z], z + 1, 1)
            high = jnp.where(lane == z, x, high)
            low = jnp.where(lane == z + 1, x, low)
        lows.append(low)
        highs.append(high)
    low = pltpu.roll(jnp.concatenate(lows, axis=0), LANES - 1, 1)
    high = jnp.concatenate(highs, axis=0)
    even_ref[3 * ROWS :] = jnp.where(x_up, high, low).T[:cells_z]
    odd_ref[3 * ROWS :] = jnp.where(x_up, low, high).T[:cells_z]


def band_kernel(tiles_x, wide, *refs):
    parts, band_ref, held = refs[:tiles_x], refs[tiles_x], refs[tiles_x + 1]
    fx = lax.axis_index("fx")
    for k, part in enumerate(parts):
        held[fx ^ k] = part[0 : 3 * ROWS]
    lane = iota((NH, wide), 1)
    at = 0
    for field in range(3):
        for t in range(NT if field < 2 else ET):
            total = None
            for f in range(tiles_x):
                x = held[f, field * ROWS : (field + 1) * ROWS]
                if wide > LANES:
                    x = jnp.concatenate([x, jnp.zeros((NH, wide - LANES), jnp.float32)], axis=1)
                shift = (EW * f - NW * t) % wide
                if shift:
                    x = pltpu.roll(x, shift, 1)
                x = jnp.where((lane >= EW * f) & (lane < EW * f + NW), x, 0.0)
                total = x if total is None else total + x
            band_ref[at : at + NH] = total
            at += NH


def air_kernel(tiles_s, tiles_x, tiles_y, air_ref, z_even, z_odd, *refs):
    refs = list(refs)
    y_even = refs.pop(0)
    y_odd = refs.pop(0) if tiles_y > 2 else None
    x_even = refs.pop(0)
    x_odds = [(m, refs.pop(0)) for m in odd_masks(tiles_x)]
    next_hbm, edge_ref, gain_ref, west_ref, east_ref, next_ref, sem = refs
    sec, fx, fy = (lax.axis_index(axis) for axis in ("sec", "fx", "fy"))
    fields, cells_z, cells_y, cells_x = air_ref.shape
    x_up = (fx & 1) == 0
    y_up = (fy & 1) == 0
    z_up = (sec & 1) == 0
    even = x_even[3 * ROWS :]
    odd = jnp.zeros_like(even)
    partner = jnp.where(x_up, fx - 1, fx + 1)
    for m, ref in x_odds:
        odd = jnp.where((fx ^ partner) == m, ref[3 * ROWS :], odd)
    pad = jnp.zeros((LANES - cells_z, LANES), jnp.float32)
    west_ref[...] = jnp.concatenate([jnp.where(x_up, odd, even), pad], axis=0).T
    east_ref[...] = jnp.concatenate([jnp.where(x_up, even, odd), pad], axis=0).T
    row = iota((cells_y, LANES), 0)
    lane = iota((cells_y, LANES), 1)
    half = 0.5 * time_step
    mix = time_step * viscosity

    def layer(z, below, above):
        u, v, w = air_ref[1, z], air_ref[2, z], air_ref[3, z]
        hu, hv, hw = half * u, half * v, half * w
        gain_ref[pl.ds(z, 1), :] = (mix + hv[0:1]) * jnp.where(fy == 0, 1.0, 0.0)
        for f in range(fields):
            x = air_ref[f, z]
            span = slice(f * cells_y, (f + 1) * cells_y)
            west = jnp.where(
                lane == 0,
                pltpu.roll(west_ref[span], (LANES - z) % LANES, 1),
                pltpu.roll(x, 1, 1),
            )
            east = jnp.where(
                lane == LANES - 1,
                pltpu.roll(east_ref[span], LANES - 1 - z, 1),
                pltpu.roll(x, LANES - 1, 1),
            )
            y_e = y_even[f, pl.ds(z, 1), :]
            y_o = y_odd[f, pl.ds(z, 1), :] if y_odd is not None else jnp.zeros_like(y_e)
            south_ghost = jnp.where(y_up, y_o, y_e)
            north_ghost = jnp.where(y_up, y_e, y_o)
            south = jnp.where(row == 0, south_ghost, pltpu.roll(x, 1, 0))
            north = jnp.where(row == cells_y - 1, north_ghost, pltpu.roll(x, cells_y - 1, 0))
            lower, upper = below(f), above(f)
            out = (
                (1.0 - 6.0 * mix) * x
                + mix * (east + west + north + south + upper + lower)
                + hu * (west - east)
                + hv * (south - north)
                + hw * (lower - upper)
            )
            next_ref[f, z] = out
            if f == 0:
                edge_ref[z] = out[:SUBS]

    def ghost_low(f):
        return jnp.where(z_up, z_odd[f], z_even[f])

    def ghost_high(f):
        return jnp.where(z_up, z_even[f], z_odd[f])

    steps = 4
    depth = cells_z // steps
    for step in range(steps):
        start, stop = step * depth, (step + 1) * depth
        if start == 0:
            layer(0, ghost_low, lambda f: air_ref[f, 1])

        @pl.loop(max(start, 1), min(stop, cells_z - 1))
        def _(z):
            layer(z, lambda f: air_ref[f, z - 1], lambda f: air_ref[f, z + 1])

        if stop == cells_z:
            layer(cells_z - 1, lambda f: air_ref[f, cells_z - 2], ghost_high)
        pltpu.make_async_copy(
            next_ref.at[:, start:stop], next_hbm.at[:, start:stop], sem
        ).start()
    pltpu.make_async_copy(next_ref, next_hbm, sem).wait()


def place_kernel(nodes_ref, iface_ref, place_ref, rows_ref):
    nodes = nodes_ref[...]
    at_row = iota(nodes.shape, 0).astype(jnp.float32)
    at_lane = iota(nodes.shape, 1).astype(jnp.float32)
    high, low = spread(nodes, [at_row, at_lane])
    place = high * LANES + low
    place_ref[...] = place.astype(jnp.int32)
    count = iface_ref.shape[-1] // LANES
    iface = jnp.concatenate(
        [iface_ref[0:1, LANES * r : LANES * (r + 1)] for r in range(count)], axis=0
    )
    rows_ref[...] = look_up([place[r : r + 1] for r in range(ROWS)], iface)


def face_kernel(tiles_y, face_ref, *refs):
    parts, wall_ref, held = refs[:tiles_y], refs[tiles_y], refs[tiles_y + 1]
    fy = lax.axis_index("fy")
    for k, part in enumerate(parts):
        held[fy ^ k] = part[...] + (fy ^ k).astype(jnp.float32) * (ROWS * LANES)
    rows = jnp.concatenate([held[j] for j in range(tiles_y)], axis=0)
    row = rows.astype(jnp.int32)
    high, low = spread(
        face_ref[...],
        [(row >> 7).astype(jnp.float32), (row & (LANES - 1)).astype(jnp.float32)],
    )
    wall_ref[...] = (high * LANES + low).astype(jnp.int32)


def solve_kernel(
    tiles_s, tiles_x, tiles_y, wide, material_count,
    conduct_ref, capacity_ref, place_ref, wall_ref, edge_ref, gain_ref, air_ref, *refs,
):
    bands = tiles_s * tiles_y
    parts = refs[:bands]
    solid_ref, next_ref = refs[bands : bands + 2]
    (held, elem, side, main, inv, res, dirn, image, sol, table, edge, solid, sem) = refs[bands + 2 :]
    sec, fx, fy = (lax.axis_index(axis) for axis in ("sec", "fx", "fy"))
    for j in range(tiles_y):
        for k in range(tiles_s):
            held[(sec ^ k) * tiles_y + (fy ^ j)] = parts[j * tiles_s + k][...]

    lane = iota((NH, wide), 1)
    first_row = iota((NH, wide), 0) == 0
    used = lane < EW * tiles_x + 1

    def right(x):
        return pltpu.roll(x, wide - 1, 1)

    def left(x):
        return pltpu.roll(x, 1, 1)

    def up(x):
        return pltpu.roll(x, NH - 1, 0)

    def down(x):
        return pltpu.roll(x, 1, 0)

    def to_nodes(x):
        x = x + left(x)
        return x + down(x)

    def seams(ref):
        for k in range(1, bands):
            for t in range(NT):
                both = ref[k - 1, t, NH - 1 : NH, :] + ref[k, t, 0:1, :]
                ref[k - 1, t, NH - 1 : NH, :] = both
                ref[k, t, 0:1, :] = both

    def each_band(body, total=None):
        for b in range(bands):
            total = body(b, total)
        return total

    def prepare(b, _):
        cells, own = [], []
        for t in range(ET):
            kind = held[b, 2 * FIELD_ROWS + t * NH : 2 * FIELD_ROWS + (t + 1) * NH, :]
            x = jnp.zeros_like(kind)
            s = jnp.zeros_like(kind)
            for m in range(material_count):
                x = jnp.where(kind == m + 1.0, conduct_ref[m] * (1.0 / 12.0), x)
                s = jnp.where(kind == m + 1.0, capacity_ref[m] * 0.125, s)
            elem[b, t] = x
            side[b, t] = to_nodes(x)
            cells.append(x)
            own.append(5.0 * x + s)
        for t in range(NT):
            if t == 0:
                m = own[0]
            elif t == NT - 1:
                m = own[ET - 1]
            else:
                m = own[t] + own[t - 1]
            main[b, t] = to_nodes(m)
            inv[b, t] = held[b, t * NH : (t + 1) * NH, :]
            res[b, t] = held[b, FIELD_ROWS + t * NH : FIELD_ROWS + (t + 1) * NH, :]
        return _

    each_band(prepare)
    seams(inv)
    seams(res)

    zero = jnp.zeros((NH, wide), jnp.float32)

    def count_once(b, x):
        return jnp.where(first_row, 0.0, x) if b else x

    def total_of(x):
        return jnp.sum(jnp.sum(x, axis=0, keepdims=True), axis=1, keepdims=True)

    def begin(b, acc):
        for t in range(NT):
            d = jnp.where(used, 1.0 / inv[b, t], 0.0)
            inv[b, t] = d
            r = res[b, t]
            z = r * d
            dirn[b, t] = z
            acc = acc + count_once(b, r * z)
        return acc

    gamma = total_of(each_band(begin, zero))

    beta = None
    for iteration in range(ITERS):

        def operate(b, acc, beta=beta):
            p, cross, diag, layer = [], [], [], []
            for t in range(NT):
                x = dirn[b, t]
                if beta is not None:
                    x = res[b, t] * inv[b, t] + beta * x
                    dirn[b, t] = x
                y = right(x)
                d = x + up(y)
                c = y + up(x)
                p.append(x)
                diag.append(d)
                cross.append(c)
                layer.append(d + c)
            for t in range(NT):
                out = main[b, t] * p[t]
                if t == 0:
                    both = elem[b, 0]
                    other = both * layer[1]
                    out = out + side[b, 0] * p[1]
                elif t == NT - 1:
                    both = elem[b, ET - 1]
                    other = both * layer[ET - 1]
                    out = out + side[b, ET - 1] * p[ET - 1]
                else:
                    both = elem[b, t] + elem[b, t - 1]
                    other = elem[b, t] * layer[t + 1] + elem[b, t - 1] * layer[t - 1]
                    out = out + side[b, t] * p[t + 1] + side[b, t - 1] * p[t - 1]
                on_diag = other + both * diag[t]
                on_cross = other + both * cross[t]
                out = out - (on_diag + left(on_cross)) - down(on_cross + left(on_diag))
                image[b, t] = out
                acc = acc + p[t] * out
            return acc

        step_len = gamma / total_of(each_band(operate, zero))
        last = iteration + 1 == ITERS
        if not last:
            seams(image)

        def update(b, acc, step_len=step_len):
            for t in range(NT):
                r = res[b, t] - step_len * image[b, t]
                res[b, t] = r
                acc = acc + count_once(b, r * r * inv[b, t])
            return acc

        for j in range(tiles_y):
            for t in range(NT):
                x = step_len * dirn[sec * tiles_y + j, t]
                sol[j, t] = x if iteration == 0 else sol[j, t] + x
        if not last:
            gamma_next = total_of(each_band(update, zero))
            beta = gamma_next / gamma
            gamma = gamma_next

    for j in range(tiles_y):
        packed = jnp.zeros((NH, LANES), jnp.float32)
        spot = iota((NH, LANES), 1) >> 5
        for t in range(NT):
            x = sol[j, t]
            x = pltpu.roll(x, (NW * t - EW * fx + tiles_x * wide) % wide, 1)[:, :LANES]
            packed = jnp.where(spot == t, x, packed)
        table[j] = packed
    solid[...] = look_up([table[fy, r : r + 1] for r in range(ROWS)], place_ref[...])
    first = pltpu.make_async_copy(solid, solid_ref, sem.at[0])
    first.start()
    rows = [table[j, r : r + 1] for j in range(tiles_y) for r in range(ROWS)]
    extra = look_up(rows, wall_ref[...]) * gain_ref[...]
    cells_z = edge_ref.shape[0]
    top = iota((SUBS, LANES), 0) == 0
    for z in range(cells_z):
        edge[z] = edge_ref[z] + jnp.where(top, extra[z : z + 1], 0.0)
    second = pltpu.make_async_copy(edge, next_ref.at[0, :, 0:SUBS, :], sem.at[1])
    second.start()
    first.wait()
    second.wait()


def odd_masks(count):
    return sorted({i ^ (i + 1) for i in range(1, count - 1, 2)})


def swap(x, axis, mask):
    count = lax.axis_size(axis)
    return lax.ppermute(x, axis, [(i, i ^ mask) for i in range(count)])


def pair_swap(x, axis, odd):
    count = lax.axis_size(axis)
    pairs = []
    for i in range(odd, count - 1, 2):
        pairs += [(i, i + 1), (i + 1, i)]
    return lax.ppermute(x, axis, pairs) if pairs else jnp.zeros_like(x)


def on_device(
    conn,
    material,
    side_nodes,
    rim_nodes,
    iface_node,
    face_of_row,
    conductivity,
    capacity,
    diag_part,
    heat_source,
    air_state,
):
    f32 = jnp.float32
    tiles_s, tiles_x, tiles_y = (lax.axis_size(axis) for axis in ("sec", "fx", "fy"))
    bands = tiles_s * tiles_y
    wide = -(-(EW * tiles_x + 1) // LANES) * LANES
    elem_lanes = -(-ELEMS // LANES) * LANES
    fields, cells_z, cells_y, cells_x = air_state.shape

    def call(kernel, args, specs, outs, out_specs, scratch=(), **more):
        held = list(args) + list(outs) + [s for s in scratch if hasattr(s, "shape")]
        need = sum(4 * int(np.prod(x.shape)) for x in held)
        return pl.pallas_call(
            kernel,
            in_specs=specs,
            out_specs=out_specs,
            out_shape=outs,
            scratch_shapes=list(scratch),
            compiler_params=pltpu.CompilerParams(vmem_limit_bytes=need + (6 << 20)),
            **more,
        )(*args)

    def shape(*dims):
        return jax.ShapeDtypeStruct(dims, f32)

    def ints(*dims):
        return jax.ShapeDtypeStruct(dims, jnp.int32)

    def whole(*dims):
        return pl.BlockSpec(dims, lambda i: (0,) * len(dims))

    plain, even, odd, nodes, y_even, y_odd, z_even, z_odd, air = call(
        stage_kernel,
        [
            conn.reshape(conn.shape[-2:]),
            material.reshape(1, -1),
            diag_part.reshape(ROWS, LANES),
            heat_source.reshape(ROWS, LANES),
            air_state,
        ],
        [
            whole(8, elem_lanes),
            whole(1, elem_lanes),
            whole(ROWS, LANES),
            whole(ROWS, LANES),
            ANY,
        ],
        [
            shape(3 * ROWS, LANES),
            shape(3 * ROWS + cells_z, LANES),
            shape(3 * ROWS + cells_z, LANES),
            ints(ROWS, LANES),
            shape(fields, cells_z, cells_x),
            shape(fields, cells_z, cells_x),
            shape(fields, cells_y, cells_x),
            shape(fields, cells_y, cells_x),
            shape(*air_state.shape),
        ],
        [VMEM] * 9,
        [pltpu.SemaphoreType.DMA],
        grid=(1,),
    )
    odds = odd_masks(tiles_x)
    pays = [plain] + [
        swap(even if k == 1 else odd if k in odds else plain, "fx", k) for k in range(1, tiles_x)
    ]
    z_even, z_odd = pair_swap(z_even, "sec", 0), pair_swap(z_odd, "sec", 1)
    y_ghosts = [pair_swap(y_even, "fy", 0)]
    if tiles_y > 2:
        y_ghosts.append(pair_swap(y_odd, "fy", 1))

    place, rows = call(
        place_kernel,
        [nodes, iface_node.reshape(1, -1)],
        [VMEM] * 2,
        [ints(ROWS, LANES), shape(iface_node.shape[-1] // LANES, LANES)],
        [VMEM] * 2,
    )

    band = call(
        lambda *refs: band_kernel(tiles_x, wide, *refs),
        pays,
        [VMEM] * tiles_x,
        [shape(BAND_ROWS, wide)],
        [VMEM],
        [pltpu.VMEM((tiles_x, 3 * ROWS, LANES), f32)],
    )[0]
    own_bands = [band] + [swap(band, "sec", k) for k in range(1, tiles_s)]
    all_bands = own_bands + [swap(b, "fy", j) for j in range(1, tiles_y) for b in own_bands]
    all_rows = [rows] + [swap(rows, "fy", j) for j in range(1, tiles_y)]

    wall = call(
        lambda *refs: face_kernel(tiles_y, *refs),
        [face_of_row.reshape(-1, LANES)] + all_rows,
        [VMEM] * (1 + tiles_y),
        [ints(cells_z, LANES)],
        [VMEM],
        [pltpu.VMEM((tiles_y,) + rows.shape, f32)],
    )[0]

    ghosts = [z_even, z_odd] + y_ghosts + [pays[1]] + [pays[m] for m in odds]
    air_next, edge, gain = call(
        lambda *refs: air_kernel(tiles_s, tiles_x, tiles_y, *refs),
        [air] + ghosts,
        [VMEM] * (1 + len(ghosts)),
        [shape(*air_state.shape), shape(cells_z, SUBS, LANES), shape(cells_z, LANES)],
        [ANY, VMEM, VMEM],
        [pltpu.VMEM((LANES, LANES), f32)] * 2
        + [pltpu.VMEM(air_state.shape, f32), pltpu.SemaphoreType.DMA],
    )

    grid = (bands, NT, NH, wide)
    solid, air_next = call(
        lambda *refs: solve_kernel(
            tiles_s, tiles_x, tiles_y, wide, conductivity.shape[0], *refs
        ),
        [conductivity, capacity, place, wall, edge, gain, air_next] + all_bands,
        [SMEM] * 2 + [VMEM] * 4 + [ANY] + [VMEM] * bands,
        [shape(ROWS, LANES), shape(*air_state.shape)],
        [ANY, ANY],
        [pltpu.VMEM((bands, BAND_ROWS, wide), f32)]
        + [pltpu.VMEM((bands, ET, NH, wide), f32)] * 2
        + [pltpu.VMEM(grid, f32)] * 5
        + [
            pltpu.VMEM((tiles_y, NT, NH, wide), f32),
            pltpu.VMEM((tiles_y, ROWS, LANES), f32),
            pltpu.VMEM((cells_z, SUBS, LANES), f32),
            pltpu.VMEM((ROWS, LANES), f32),
            pltpu.SemaphoreType.DMA((2,)),
        ],
        input_output_aliases={6: 1},
    )
    return solid.reshape(diag_part.shape), air_next


def solution(mesh):
    return jax.shard_map(
        on_device,
        mesh=mesh,
        in_specs=(
            P("sec", "fx", "fy", None, None),
            P("sec", "fx", "fy", None),
            P("sec", "fx", "fy", None, None),
            P("sec", "fx", "fy", None, None),
            P("sec", "fx", "fy", None),
            P("sec", "fx", None),
            P(),
            P(),
            P("sec", "fx", "fy", None),
            P("sec", "fx", "fy", None),
            P(None, "sec", "fy", "fx"),
        ),
        out_specs=(P("sec", "fx", "fy", None), P(None, "sec", "fy", "fx")),
        check_vma=False,
    )
```

```python
import jax
import jax.numpy as jnp
import numpy as np
from jax import lax
from jax.experimental import pallas as pl
from jax.experimental.pallas import tpu as pltpu
from jax.sharding import PartitionSpec as P

NW = 32
NH = 24
NT = 4
ITERS = 4
LANES = 128
SUBS = 8

time_step = 0.2
viscosity = 0.75

VMEM = pl.BlockSpec(memory_space=pltpu.VMEM)
SMEM = pl.BlockSpec(memory_space=pltpu.SMEM)
ANY = pl.BlockSpec(memory_space=pl.ANY)
HBM = pl.BlockSpec(memory_space=pltpu.HBM)

EW = NW - 1
EH = NH - 1
ET = NT - 1
ELEMS = ET * EH * EW
ROWS = NT * NH * NW // LANES
FIELD_ROWS = NT * NH
BAND_ROWS = 2 * FIELD_ROWS + ET * NH


def iota(shape, dim):
    return lax.broadcasted_iota(jnp.int32, shape, dim)


def lane_pick(row, idx):
    return jnp.take_along_axis(
        jnp.broadcast_to(row, idx.shape), idx, axis=1, mode="promise_in_bounds"
    )


def look_up(load, count, place):
    outs = []
    for start in range(0, place.shape[0], SUBS):
        part = place[start : start + SUBS]
        high = part >> 7
        low = part & (LANES - 1)
        out = None
        for r in range(count):
            got = lane_pick(load(r), low)
            out = got if out is None else jnp.where(high == r, got, out)
        outs.append(out)
    return jnp.concatenate(outs, axis=0) if len(outs) > 1 else outs[0]


def spread(idx, values):
    count = idx.shape[0]
    acc = None
    group = 4
    for start in range(0, count, group):
        left, right = [], []
        for r in range(start, start + group):
            row = idx[r : r + 1]
            hot_high = iota((count, LANES), 0) == (row >> 7)
            hot_low = iota((LANES, LANES), 0) == (row & (LANES - 1))
            left.append(
                jnp.concatenate(
                    [jnp.where(hot_high, v[r : r + 1], 0.0) for v in values], axis=0
                ).astype(jnp.bfloat16)
            )
            right.append(jnp.where(hot_low, 1.0, 0.0).astype(jnp.bfloat16))
        part = lax.dot_general(
            jnp.concatenate(left, axis=1),
            jnp.concatenate(right, axis=1),
            (((1,), (1,)), ((), ())),
            preferred_element_type=jnp.float32,
        )
        acc = part if acc is None else acc + part
    return [acc[i * count : (i + 1) * count] for i in range(len(values))]


def element_keys():
    h = np.arange(NH)[:, None]
    lane = np.arange(LANES)[None, :]
    t, w = lane // NW, lane % NW
    corner = 4 * (t == NT - 1) + 2 * (h == NH - 1) + (w == NW - 1)
    column = np.minimum(t, ET - 1) * EH * EW + np.minimum(h, EH - 1) * EW + np.minimum(w, EW - 1)
    return corner, column


def stage_kernel(
    conn_hbm, material_hbm, diag_hbm, source_hbm, air_hbm,
    plain_ref, even_ref, odd_ref, nodes_ref, y_even, y_odd, z_even, z_odd, air_ref,
    conn_ref, material_ref, diag_ref, source_ref, sem,
):
    sec, fx, fy = (lax.axis_index(axis) for axis in ("sec", "fx", "fy"))
    loads = [
        pltpu.make_async_copy(a, b, sem.at[i])
        for i, (a, b) in enumerate(
            [
                (conn_hbm, conn_ref),
                (diag_hbm, diag_ref),
                (source_hbm, source_ref),
                (material_hbm, material_ref),
                (air_hbm, air_ref),
            ]
        )
    ]
    for load in loads:
        load.start()
    corner_np, column_np = element_keys()
    last = ELEMS // LANES

    def column_tile(ref, c, k):
        start = ELEMS - LANES if k == last else LANES * k
        return ref[c : c + 1, start : start + LANES]

    loads[0].wait()
    loads[3].wait()
    pieces, kinds = [], []
    for j in range(NH // SUBS):
        h = iota((SUBS, LANES), 0) + SUBS * j
        lane = iota((SUBS, LANES), 1)
        t = lane >> 5
        w = lane & (NW - 1)
        corner = (
            jnp.where(t == NT - 1, 4, 0) + jnp.where(h == NH - 1, 2, 0) + jnp.where(w == NW - 1, 1, 0)
        )
        column = (
            jnp.minimum(t, ET - 1) * (EH * EW)
            + jnp.minimum(h, EH - 1) * EW
            + jnp.minimum(w, EW - 1)
        )
        tile = column >> 7
        low = jnp.where(tile == last, column - (ELEMS - LANES), column & (LANES - 1))
        key = tile * 8 + corner
        rows = slice(SUBS * j, SUBS * (j + 1))
        wanted = sorted(set((column_np[rows] // LANES * 8 + corner_np[rows]).reshape(-1).tolist()))
        out = jnp.zeros((SUBS, LANES), jnp.int32)
        for code in wanted:
            c, k = code % 8, code // 8
            out = jnp.where(key == code, lane_pick(column_tile(conn_ref, c, k), low), out)
        pieces.append(out)
        kind = jnp.full((SUBS, LANES), -1, jnp.int32)
        for k in sorted({code // 8 for code in wanted if code % 8 == 0}):
            row = column_tile(material_ref, 0, k)
            kind = jnp.where((corner == 0) & (tile == k), lane_pick(row, low), kind)
        kinds.append(kind)
    nodes = jnp.concatenate(pieces, axis=0)
    nodes_ref[...] = nodes
    loads[1].wait()
    loads[2].wait()
    diag = look_up(lambda r: diag_ref[r : r + 1], ROWS, nodes)
    source = look_up(lambda r: source_ref[r : r + 1], ROWS, nodes)
    kind = jnp.concatenate(kinds, axis=0).astype(jnp.float32) + 1.0
    for ref in (plain_ref, even_ref, odd_ref):
        ref[0:ROWS] = diag
        ref[ROWS : 2 * ROWS] = source
        ref[2 * ROWS : 3 * ROWS] = kind

    loads[4].wait()
    fields, cells_z, cells_y, cells_x = air_ref.shape
    z_up = (sec & 1) == 0
    z_even[...] = air_ref[:, jnp.where(z_up, cells_z - 1, 0)]
    z_odd[...] = air_ref[:, jnp.where(z_up, 0, cells_z - 1)]
    y_up = (fy & 1) == 0
    x_up = (fx & 1) == 0
    lane = iota((cells_y, LANES), 1)
    lows, highs = [], []
    for f in range(fields):
        first = air_ref[f, :, 0, :]
        last = air_ref[f, :, cells_y - 1, :]
        y_even[f] = jnp.where(y_up, last, first)
        y_odd[f] = jnp.where(y_up, first, last)
        low = jnp.zeros((cells_y, LANES), jnp.float32)
        high = jnp.zeros((cells_y, LANES), jnp.float32)
        for z in range(cells_z):
            x = pltpu.roll(air_ref[f, z], z + 1, 1)
            high = jnp.where(lane == z, x, high)
            low = jnp.where(lane == z + 1, x, low)
        lows.append(low)
        highs.append(high)
    low = pltpu.roll(jnp.concatenate(lows, axis=0), LANES - 1, 1)
    high = jnp.concatenate(highs, axis=0)
    even_ref[3 * ROWS :] = jnp.where(x_up, high, low).T[:cells_z]
    odd_ref[3 * ROWS :] = jnp.where(x_up, low, high).T[:cells_z]


def band_kernel(tiles_x, wide, *refs):
    parts, (rows_ref, z_even, z_odd) = refs[:tiles_x], refs[tiles_x : tiles_x + 3]
    plain_ref, even_ref, odd_ref, both_ref, held = refs[-5:]
    both_ref[BAND_ROWS : BAND_ROWS + rows_ref.shape[0], :LANES] = rows_ref[...]
    fields, cells_y = z_even.shape[:2]
    for f in range(fields):
        span = slice(BAND_ROWS + f * cells_y, BAND_ROWS + (f + 1) * cells_y)
        even_ref[span, :LANES] = z_even[f]
        odd_ref[span, :LANES] = z_odd[f]
    fx = lax.axis_index("fx")
    for k, part in enumerate(parts):
        held[fx ^ k] = part[0 : 3 * ROWS]
    lane = iota((NH, wide), 1)
    at = 0
    for field in range(3):
        for t in range(NT if field < 2 else ET):
            total = None
            for f in range(tiles_x):
                x = held[f, field * ROWS : (field + 1) * ROWS]
                if wide > LANES:
                    x = jnp.concatenate([x, jnp.zeros((NH, wide - LANES), jnp.float32)], axis=1)
                shift = (EW * f - NW * t) % wide
                if shift:
                    x = pltpu.roll(x, shift, 1)
                x = jnp.where((lane >= EW * f) & (lane < EW * f + NW), x, 0.0)
                total = x if total is None else total + x
            for ref in (plain_ref, even_ref, odd_ref, both_ref):
                ref[at : at + NH] = total
            at += NH


def air_kernel(tiles_x, tiles_y, air_ref, *refs):
    refs = list(refs)
    y_even = refs.pop(0)
    y_odd = refs.pop(0) if tiles_y > 2 else None
    x_even = refs.pop(0)
    x_odds = [(m, refs.pop(0)) for m in odd_masks(tiles_x)]
    next_hbm, edge_ref, gain_ref, ends_ref, weight_ref, west_ref, east_ref, next_ref, sem = refs
    fx, fy = lax.axis_index("fx"), lax.axis_index("fy")
    fields, cells_z, cells_y, cells_x = air_ref.shape
    x_up = (fx & 1) == 0
    y_up = (fy & 1) == 0
    even = x_even[3 * ROWS :]
    odd = jnp.zeros_like(even)
    partner = jnp.where(x_up, fx - 1, fx + 1)
    for m, ref in x_odds:
        odd = jnp.where((fx ^ partner) == m, ref[3 * ROWS :], odd)
    pad = jnp.zeros((LANES - cells_z, LANES), jnp.float32)
    west_ref[...] = jnp.concatenate([jnp.where(x_up, odd, even), pad], axis=0).T
    east_ref[...] = jnp.concatenate([jnp.where(x_up, even, odd), pad], axis=0).T
    row = iota((cells_y, LANES), 0)
    lane = iota((cells_y, LANES), 1)
    half = 0.5 * time_step
    mix = time_step * viscosity

    def layer(z, below, above):
        u, v, w = air_ref[1, z], air_ref[2, z], air_ref[3, z]
        hu, hv, hw = half * u, half * v, half * w
        gain_ref[pl.ds(z, 1), :] = (mix + hv[0:1]) * jnp.where(fy == 0, 1.0, 0.0)
        for f in range(fields):
            x = air_ref[f, z]
            span = slice(f * cells_y, (f + 1) * cells_y)
            west = jnp.where(
                lane == 0,
                pltpu.roll(west_ref[span], (LANES - z) % LANES, 1),
                pltpu.roll(x, 1, 1),
            )
            east = jnp.where(
                lane == LANES - 1,
                pltpu.roll(east_ref[span], LANES - 1 - z, 1),
                pltpu.roll(x, LANES - 1, 1),
            )
            y_e = y_even[f, pl.ds(z, 1), :]
            y_o = y_odd[f, pl.ds(z, 1), :] if y_odd is not None else jnp.zeros_like(y_e)
            south_ghost = jnp.where(y_up, y_o, y_e)
            north_ghost = jnp.where(y_up, y_e, y_o)
            south = jnp.where(row == 0, south_ghost, pltpu.roll(x, 1, 0))
            north = jnp.where(row == cells_y - 1, north_ghost, pltpu.roll(x, cells_y - 1, 0))
            lower, upper = below(f), above(f)
            out = (
                (1.0 - 6.0 * mix) * x
                + mix * (east + west + north + south + upper + lower)
                + hu * (west - east)
                + hv * (south - north)
                + hw * (lower - upper)
            )
            next_ref[f, z] = out
            if f == 0:
                edge_ref[z] = out[:SUBS]

    def outside(f):
        return jnp.zeros((cells_y, LANES), jnp.float32)

    steps = 4
    depth = cells_z // steps
    for step in range(steps):
        start, stop = step * depth, (step + 1) * depth
        if start == 0:
            layer(0, outside, lambda f: air_ref[f, 1])

        @pl.loop(max(start, 1), min(stop, cells_z - 1))
        def _(z):
            layer(z, lambda f: air_ref[f, z - 1], lambda f: air_ref[f, z + 1])

        if stop == cells_z:
            layer(cells_z - 1, lambda f: air_ref[f, cells_z - 2], outside)
        pltpu.make_async_copy(
            next_ref.at[:, start:stop], next_hbm.at[:, start:stop], sem
        ).start()
    for i, z in enumerate((0, cells_z - 1)):
        hw = half * air_ref[3, z]
        weight_ref[i] = mix - hw if i else mix + hw
        ends_ref[i] = next_ref[:, z]
    pltpu.make_async_copy(next_ref, next_hbm, sem).wait()


def place_kernel(nodes_ref, iface_ref, place_ref, rows_ref):
    nodes = nodes_ref[...]
    at_row = iota(nodes.shape, 0).astype(jnp.float32)
    at_lane = iota(nodes.shape, 1).astype(jnp.float32)
    high, low = spread(nodes, [at_row, at_lane])
    place = high * LANES + low
    place_ref[...] = place.astype(jnp.int32)
    count = iface_ref.shape[-1] // LANES
    iface = jnp.concatenate(
        [iface_ref[0:1, LANES * r : LANES * (r + 1)] for r in range(count)], axis=0
    )
    rows_ref[...] = look_up(lambda r: place[r : r + 1], ROWS, iface)


def face_kernel(tiles_y, face_ref, *refs):
    parts, wall_ref, held = refs[:tiles_y], refs[tiles_y], refs[tiles_y + 1]
    fy = lax.axis_index("fy")
    for k, part in enumerate(parts):
        count = held.shape[1]
        rows = part[BAND_ROWS : BAND_ROWS + count, :LANES]
        held[fy ^ k] = rows + (fy ^ k).astype(jnp.float32) * (ROWS * LANES)
    rows = jnp.concatenate([held[j] for j in range(tiles_y)], axis=0)
    row = rows.astype(jnp.int32)
    high, low = spread(
        face_ref[...],
        [(row >> 7).astype(jnp.float32), (row & (LANES - 1)).astype(jnp.float32)],
    )
    wall_ref[...] = (high * LANES + low).astype(jnp.int32)


def solve_kernel(
    tiles_s, tiles_x, tiles_y, wide, material_count,
    conduct_ref, capacity_ref, place_ref, wall_ref, edge_ref, gain_ref, ends_ref, weight_ref, air_ref,
    *refs,
):
    bands = tiles_s * tiles_y
    parts = refs[:bands]
    solid_ref, next_ref = refs[bands : bands + 2]
    (held, elem, side, main, inv, res, dirn, image, sol, table, last_table, edge, solid, ends, sem) = refs[
        bands + 2 :
    ]
    sec, fx, fy = (lax.axis_index(axis) for axis in ("sec", "fx", "fy"))
    z_up = (sec & 1) == 0
    fields, cells_z, cells_y = air_ref.shape[:3]
    z_odds = [(m, parts[m]) for m in odd_masks(tiles_s)]
    across = sec ^ jnp.where(z_up, sec - 1, sec + 1)
    outer = [
        pltpu.make_async_copy(ends.at[i], next_ref.at[:, z], sem.at[2 + i])
        for i, z in enumerate((0, cells_z - 1))
    ]
    lane_tiles = [slice(i, i + LANES) for i in range(0, wide, LANES)]

    @pl.when(fy >= 0)
    def _():
        for i, copy in enumerate(outer):
            for f in range(fields):
                span = slice(BAND_ROWS + f * cells_y, BAND_ROWS + (f + 1) * cells_y)
                even = parts[1][span, :LANES]
                odd = jnp.zeros_like(even)
                for m, part in z_odds:
                    odd = jnp.where(across == m, part[span, :LANES], odd)
                here, there = (odd, even) if i == 0 else (even, odd)
                ends[i, f] = ends_ref[i, f] + weight_ref[i] * jnp.where(z_up, here, there)
            copy.start()

    @pl.when(fy >= 0)
    def _():
        for j in range(tiles_y):
            for k in range(tiles_s):
                band = (sec ^ k) * tiles_y + (fy ^ j)
                for i, cut in enumerate(lane_tiles):
                    held[i, pl.ds(band, BAND_ROWS, stride=bands), :] = parts[j * tiles_s + k][
                        0:BAND_ROWS, cut
                    ]

    def loop(start, stop, body, carry):
        if bands * wide > SUBS * LANES:
            return lax.fori_loop(start, stop, body, carry)
        for h in range(start, stop):
            carry = body(h, carry)
        return carry

    def span_of(r):
        return pl.ds(r * bands if isinstance(r, int) else pl.multiple_of(r * bands, bands), bands)

    def join(tiles):
        return tiles[0] if len(tiles) == 1 else jnp.concatenate(tiles, axis=1)

    def row_of(ref, r):
        return join([ref[i, span_of(r), :] for i in range(len(lane_tiles))])

    def put(ref, r, x):
        for i, cut in enumerate(lane_tiles):
            ref[i, span_of(r), :] = x[:, cut]

    lane = iota((bands, wide), 1)
    band = iota((bands, wide), 0)
    used = lane < EW * tiles_x + 1

    def right(x):
        return pltpu.roll(x, wide - 1, 1)

    def left(x):
        return pltpu.roll(x, 1, 1)

    def plus(*terms):
        terms = [x for x in terms if x is not None]
        total = terms[0] if terms else None
        for x in terms[1:]:
            total = total + x
        return total

    def seam(low, high):
        below = jnp.where(band > 0, pltpu.roll(high, 1, 0), 0.0)
        above = jnp.where(band < bands - 1, pltpu.roll(low, bands - 1, 0), 0.0)
        return low + below, high + above

    def total_of(parts):
        x = plus(*parts)
        return jnp.sum(jnp.sum(x, axis=0, keepdims=True), axis=1, keepdims=True)

    def first_row(ref, x, n):
        return seam(x, row_of(ref, n + NH - 1))[0]

    def last_row(ref, x, n):
        return seam(row_of(ref, n - NH + 1), x)[1]

    def once(x):
        return jnp.where(band > 0, 0.0, x)

    zero = jnp.zeros((bands, wide), jnp.float32)

    @pl.when(fy >= 0)
    def _():
        def prepare(h, before):
            now = []
            for t in range(ET):
                kind = row_of(held, 2 * FIELD_ROWS + t * NH + h)
                x = jnp.zeros_like(kind)
                s = jnp.zeros_like(kind)
                for m in range(material_count):
                    x = jnp.where(kind == m + 1.0, conduct_ref[m] * (1.0 / 12.0), x)
                    s = jnp.where(kind == m + 1.0, capacity_ref[m] * 0.125, s)
                put(elem, t * NH + h, x)
                now += [x, 5.0 * x + s]
            both = [a + b for a, b in zip(now, before)]
            for t in range(NT):
                if t < ET:
                    x = both[2 * t]
                    put(side, t * NH + h, x + left(x))
                x = plus(both[2 * t + 1] if t < ET else None, both[2 * t - 1] if t else None)
                put(main, t * NH + h, x + left(x))
            return tuple(now)

        loop(0, NH, prepare, (zero,) * (2 * ET))

    def begin(h, acc, fix=None):
        out = []
        for t in range(NT):
            n = t * NH + h
            d, r = row_of(held, n), row_of(held, FIELD_ROWS + n)
            if fix is not None:
                d, r = fix(held, d, n), fix(held, r, FIELD_ROWS + n)
            v = jnp.where(used, 1.0 / d, 0.0)
            z = r * v
            put(inv, n, v)
            put(res, n, r)
            put(dirn, n, z)
            out.append(acc[t] + (once(r * z) if fix is first_row else r * z))
        return tuple(out)

    acc = begin(0, (zero,) * NT, first_row)
    acc = begin(NH - 1, acc, last_row)
    acc = loop(1, NH - 1, begin, acc)
    gamma = total_of(acc)

    def operate(iteration, beta, step_len):
        last = iteration + 1 == ITERS

        def fetch(h):
            p, y = [], []
            for t in range(NT):
                n = t * NH + h
                x = row_of(dirn, n)
                if beta is not None:
                    put(sol, n, plus(step_len * x, row_of(sol, n) if iteration > 1 else None))
                    x = row_of(res, n) * row_of(inv, n) + beta * x
                    put(dirn, n, x)
                p.append(x)
                y.append(right(x))
            return p, y

        def finish(h, p, diag_now, cross_now, on_diag, on_cross, acc):
            out_acc = []
            for t in range(NT):
                n = t * NH + h
                out = row_of(main, n) * p[t]
                if t < ET:
                    out = out + row_of(side, n) * p[t + 1]
                if t > 0:
                    out = out + row_of(side, n - NH) * p[t - 1]
                out = out - plus(
                    diag_now[t], on_cross[t], left(plus(cross_now[t], on_diag[t]))
                )
                if not last:
                    put(image, n, out)
                out_acc.append(acc[t] + p[t] * out)
            return out_acc

        def body(h, carry):
            p, y, on_diag, on_cross, acc = (carry[i * NT : (i + 1) * NT] for i in range(5))
            p_next, y_next = fetch(h + 1)
            diag = [p[t] + y_next[t] for t in range(NT)]
            cross = [y[t] + p_next[t] for t in range(NT)]
            layer = [a + b for a, b in zip(diag, cross)]
            x = [row_of(elem, t * NH + h) for t in range(ET)]
            diag_now, cross_now = [], []
            for t in range(NT):
                upper = x[t] if t < ET else None
                lower = x[t - 1] if t > 0 else None
                both = plus(upper, lower)
                other = plus(
                    upper * layer[t + 1] if t < ET else None,
                    lower * layer[t - 1] if t > 0 else None,
                )
                diag_now.append(other + both * diag[t])
                cross_now.append(other + both * cross[t])
            acc = finish(h, p, diag_now, cross_now, on_diag, on_cross, acc)
            return (*p_next, *y_next, *diag_now, *cross_now, *acc)

        p, y = fetch(0)
        carry = loop(0, EH, body, (*p, *y) + (zero,) * (3 * NT))
        p, y, on_diag, on_cross, acc = (carry[i * NT : (i + 1) * NT] for i in range(5))
        none = [None] * NT
        acc = finish(EH, p, none, none, on_diag, on_cross, acc)
        if last:
            for j in range(tiles_y):
                table[j] = pack(sol, j)
                last_table[j] = pack(dirn, j)
        return total_of(acc)

    spot = iota((NH, LANES), 1) >> 5

    def pack(ref, j):
        packed = None
        for t in range(NT):
            start = t * NH * bands + sec * tiles_y + j
            x = join(
                [ref[i, pl.ds(start, NH, stride=bands), :] for i in range(len(lane_tiles))]
            )
            x = pltpu.roll(x, (NW * t - EW * fx + tiles_x * wide) % wide, 1)[:, :LANES]
            packed = x if packed is None else jnp.where(spot == t, x, packed)
        return packed

    beta = step_len = None
    for iteration in range(ITERS):
        step_len = gamma / operate(iteration, beta, step_len)
        if iteration + 1 == ITERS:
            break

        def update(h, acc, fix=None, step_len=step_len):
            out = []
            for t in range(NT):
                n = t * NH + h
                q = row_of(image, n)
                if fix is not None:
                    q = fix(image, q, n)
                r = row_of(res, n) - step_len * q
                put(res, n, r)
                part = r * r * row_of(inv, n)
                out.append(acc[t] + (once(part) if fix is first_row else part))
            return tuple(out)

        acc = update(0, (zero,) * NT, first_row)
        acc = update(NH - 1, acc, last_row)
        gamma_next = total_of(loop(1, NH - 1, update, acc))
        beta = gamma_next / gamma
        gamma = gamma_next

    for j in range(tiles_y):
        table[j] = table[j] + step_len * last_table[j]
    last_table[0] = table[fy]
    first = pltpu.make_async_copy(solid, solid_ref, sem.at[0])
    second = pltpu.make_async_copy(edge, next_ref.at[0, :, 0:SUBS, :], sem.at[1])

    @pl.when(fy >= 0)
    def _():
        solid[...] = look_up(lambda r: last_table[0, r : r + 1], ROWS, place_ref[...])
        first.start()

    for copy in outer:
        copy.wait()

    @pl.when(fy == 0)
    def _():
        extra = look_up(
            lambda r: table[r // ROWS, r % ROWS : r % ROWS + 1], tiles_y * ROWS, wall_ref[...]
        )
        extra = extra * gain_ref[...]
        top = iota((SUBS, LANES), 0) == 0
        for z in range(cells_z):
            base = ends[z // (cells_z - 1), 0, :SUBS] if z in (0, cells_z - 1) else edge_ref[z]
            edge[z] = base + jnp.where(top, extra[z : z + 1], 0.0)
        second.start()
        second.wait()

    first.wait()


def odd_masks(count):
    return sorted({i ^ (i + 1) for i in range(1, count - 1, 2)})


def swap(x, axis, mask):
    count = lax.axis_size(axis)
    return lax.ppermute(x, axis, [(i, i ^ mask) for i in range(count)])


def pair_swap(x, axis, odd):
    count = lax.axis_size(axis)
    pairs = []
    for i in range(odd, count - 1, 2):
        pairs += [(i, i + 1), (i + 1, i)]
    return lax.ppermute(x, axis, pairs) if pairs else jnp.zeros_like(x)


def on_device(
    conn,
    material,
    side_nodes,
    rim_nodes,
    iface_node,
    face_of_row,
    conductivity,
    capacity,
    diag_part,
    heat_source,
    air_state,
):
    f32 = jnp.float32
    tiles_s, tiles_x, tiles_y = (lax.axis_size(axis) for axis in ("sec", "fx", "fy"))
    bands = tiles_s * tiles_y
    wide = -(-(EW * tiles_x + 1) // LANES) * LANES
    fields, cells_z, cells_y, cells_x = air_state.shape

    def call(kernel, args, specs, outs, out_specs, scratch=(), **more):
        held = list(args) + list(outs) + [s for s in scratch if hasattr(s, "shape")]
        need = sum(4 * int(np.prod(x.shape)) for x in held)
        return pl.pallas_call(
            kernel,
            in_specs=specs,
            out_specs=out_specs,
            out_shape=outs,
            scratch_shapes=list(scratch),
            compiler_params=pltpu.CompilerParams(vmem_limit_bytes=need + (6 << 20)),
            **more,
        )(*args)

    def cost(microseconds):
        return pl.CostEstimate(
            flops=0, bytes_accessed=int(3.7e6 * microseconds), transcendentals=0
        )

    def shape(*dims):
        return jax.ShapeDtypeStruct(dims, f32)

    def ints(*dims):
        return jax.ShapeDtypeStruct(dims, jnp.int32)

    plain, even, odd, nodes, y_even, y_odd, z_even, z_odd, air = call(
        stage_kernel,
        [
            pltpu.with_memory_space_constraint(x, pltpu.HBM)
            for x in (
                conn.reshape(conn.shape[-2:]),
                material.reshape(1, -1),
                diag_part.reshape(ROWS, LANES),
                heat_source.reshape(ROWS, LANES),
                air_state,
            )
        ],
        [HBM] * 5,
        [
            shape(3 * ROWS, LANES),
            shape(3 * ROWS + cells_z, LANES),
            shape(3 * ROWS + cells_z, LANES),
            ints(ROWS, LANES),
            shape(fields, cells_z, cells_x),
            shape(fields, cells_z, cells_x),
            shape(fields, cells_y, cells_x),
            shape(fields, cells_y, cells_x),
            shape(*air_state.shape),
        ],
        [VMEM] * 9,
        [
            pltpu.VMEM(conn.shape[-2:], jnp.int32),
            pltpu.VMEM((1, material.shape[-1]), jnp.int32),
            pltpu.VMEM((ROWS, LANES), f32),
            pltpu.VMEM((ROWS, LANES), f32),
            pltpu.SemaphoreType.DMA((5,)),
        ],
    )
    odds = odd_masks(tiles_x)
    pays = [plain] + [
        swap(even if k == 1 else odd if k in odds else plain, "fx", k) for k in range(1, tiles_x)
    ]
    y_ghosts = [pair_swap(y_even, "fy", 0)]
    if tiles_y > 2:
        y_ghosts.append(pair_swap(y_odd, "fy", 1))

    place, rows = call(
        place_kernel,
        [nodes, iface_node.reshape(1, -1)],
        [VMEM] * 2,
        [ints(ROWS, LANES), shape(iface_node.shape[-1] // LANES, LANES)],
        [VMEM] * 2,
        cost_estimate=cost(0.6),
    )

    ghosts = list(y_ghosts)
    plain, even, odd, both = call(
        lambda *refs: band_kernel(tiles_x, wide, *refs),
        pays + [rows, z_even, z_odd] + ghosts,
        [VMEM] * (tiles_x + 3) + [ANY] * len(ghosts),
        [shape(BAND_ROWS, wide)]
        + [shape(BAND_ROWS + fields * cells_y, wide)] * 2
        + [shape(BAND_ROWS + 2 * SUBS, wide)],
        [VMEM] * 4,
        [pltpu.VMEM((tiles_x, 3 * ROWS, LANES), f32)],
        cost_estimate=cost(0.3),
    )
    z_odds = odd_masks(tiles_s)
    own_bands = [plain] + [
        swap(even if k == 1 else odd if k in z_odds else plain, "sec", k) for k in range(1, tiles_s)
    ]
    boths = [both] + [swap(both, "fy", j) for j in range(1, tiles_y)]
    wall = call(
        lambda *refs: face_kernel(tiles_y, *refs),
        [face_of_row.reshape(-1, LANES)] + boths,
        [VMEM] * (1 + tiles_y),
        [ints(cells_z, LANES)],
        [VMEM],
        [pltpu.VMEM((tiles_y,) + rows.shape, f32)],
        cost_estimate=cost(0.5),
    )[0]

    ghosts += [pays[1]] + [pays[m] for m in odds]
    air_next, edge, gain, ends, weight = call(
        lambda *refs: air_kernel(tiles_x, tiles_y, *refs),
        [air] + ghosts,
        [VMEM] * (1 + len(ghosts)),
        [
            shape(*air_state.shape),
            shape(cells_z, SUBS, LANES),
            shape(cells_z, LANES),
            shape(2, fields, cells_y, cells_x),
            shape(2, cells_y, cells_x),
        ],
        [ANY] + [VMEM] * 4,
        [pltpu.VMEM((LANES, LANES), f32)] * 2
        + [pltpu.VMEM(air_state.shape, f32), pltpu.SemaphoreType.DMA],
        cost_estimate=cost(4.0),
    )

    marks = [edge, gain, ends]
    for k in range(1, tiles_s):
        i = (k - 1) % len(marks)
        own_bands[k], marks[i] = lax.optimization_barrier((own_bands[k], marks[i]))
    edge, gain, ends = marks
    all_bands = list(own_bands)
    for j in range(1, tiles_y):
        all_bands += [boths[j]] + [swap(b, "fy", j) for b in own_bands[1:]]

    grid = (wide // LANES, NT * NH * bands, LANES)
    solid, air_next = call(
        lambda *refs: solve_kernel(
            tiles_s, tiles_x, tiles_y, wide, conductivity.shape[0], *refs
        ),
        [conductivity, capacity, place, wall, edge, gain, ends, weight, air_next]
        + all_bands,
        [SMEM] * 2 + [VMEM] * 6 + [ANY] + [VMEM] * bands,
        [shape(ROWS, LANES), shape(*air_state.shape)],
        [ANY, ANY],
        [pltpu.VMEM((wide // LANES, BAND_ROWS * bands, LANES), f32)]
        + [pltpu.VMEM(grid, f32)] * 8
        + [
            pltpu.VMEM((tiles_y, ROWS, LANES), f32),
            pltpu.VMEM((tiles_y, ROWS, LANES), f32),
            pltpu.VMEM((cells_z, SUBS, LANES), f32),
            pltpu.VMEM((ROWS, LANES), f32),
            pltpu.VMEM((2, fields, cells_y, cells_x), f32),
            pltpu.SemaphoreType.DMA((4,)),
        ],
        input_output_aliases={8: 1},
    )
    return solid.reshape(diag_part.shape), air_next


def solution(mesh):
    return jax.shard_map(
        on_device,
        mesh=mesh,
        in_specs=(
            P("sec", "fx", "fy", None, None),
            P("sec", "fx", "fy", None),
            P("sec", "fx", "fy", None, None),
            P("sec", "fx", "fy", None, None),
            P("sec", "fx", "fy", None),
            P("sec", "fx", None),
            P(),
            P(),
            P("sec", "fx", "fy", None),
            P("sec", "fx", "fy", None),
            P(None, "sec", "fy", "fx"),
        ),
        out_specs=(P("sec", "fx", "fy", None), P(None, "sec", "fy", "fx")),
        check_vma=False,
    )
```

```python
import jax
import jax.numpy as jnp
import numpy as np
from jax import lax
from jax.experimental import pallas as pl
from jax.experimental.pallas import tpu as pltpu
from jax.sharding import PartitionSpec as P

NW = 32
NH = 24
NT = 4
ITERS = 4
LANES = 128
SUBS = 8

time_step = 0.2
viscosity = 0.75

VMEM = pl.BlockSpec(memory_space=pltpu.VMEM)
SMEM = pl.BlockSpec(memory_space=pltpu.SMEM)
ANY = pl.BlockSpec(memory_space=pl.ANY)
HBM = pl.BlockSpec(memory_space=pltpu.HBM)

EW = NW - 1
EH = NH - 1
ET = NT - 1
ELEMS = ET * EH * EW
ROWS = NT * NH * NW // LANES
FIELD_ROWS = NT * NH
BAND_ROWS = 2 * FIELD_ROWS + ET * NH


def iota(shape, dim):
    return lax.broadcasted_iota(jnp.int32, shape, dim)


def lane_pick(row, idx):
    return jnp.take_along_axis(
        jnp.broadcast_to(row, idx.shape), idx, axis=1, mode="promise_in_bounds"
    )


def look_up(load, count, place):
    outs = []
    for start in range(0, place.shape[0], SUBS):
        part = place[start : start + SUBS]
        high = part >> 7
        low = part & (LANES - 1)
        out = None
        for r in range(count):
            got = lane_pick(load(r), low)
            out = got if out is None else jnp.where(high == r, got, out)
        outs.append(out)
    return jnp.concatenate(outs, axis=0) if len(outs) > 1 else outs[0]


def spread(idx, values):
    count = idx.shape[0]
    acc = None
    group = 4
    for start in range(0, count, group):
        left, right = [], []
        for r in range(start, start + group):
            row = idx[r : r + 1]
            hot_high = iota((count, LANES), 0) == (row >> 7)
            hot_low = iota((LANES, LANES), 0) == (row & (LANES - 1))
            left.append(
                jnp.concatenate(
                    [jnp.where(hot_high, v[r : r + 1], 0.0) for v in values], axis=0
                ).astype(jnp.bfloat16)
            )
            right.append(jnp.where(hot_low, 1.0, 0.0).astype(jnp.bfloat16))
        part = lax.dot_general(
            jnp.concatenate(left, axis=1),
            jnp.concatenate(right, axis=1),
            (((1,), (1,)), ((), ())),
            preferred_element_type=jnp.float32,
        )
        acc = part if acc is None else acc + part
    return [acc[i * count : (i + 1) * count] for i in range(len(values))]


def element_keys():
    h = np.arange(NH)[:, None]
    lane = np.arange(LANES)[None, :]
    t, w = lane // NW, lane % NW
    corner = 4 * (t == NT - 1) + 2 * (h == NH - 1) + (w == NW - 1)
    column = np.minimum(t, ET - 1) * EH * EW + np.minimum(h, EH - 1) * EW + np.minimum(w, EW - 1)
    return corner, column


def stage_kernel(
    conn_hbm, material_hbm, diag_hbm, source_hbm, air_hbm,
    even_ref, odd_ref, nodes_ref, air_ref,
    conn_ref, material_ref, diag_ref, source_ref, sem,
):
    fx = lax.axis_index("fx")
    loads = [
        pltpu.make_async_copy(a, b, sem.at[i])
        for i, (a, b) in enumerate(
            [
                (conn_hbm, conn_ref),
                (diag_hbm, diag_ref),
                (source_hbm, source_ref),
                (material_hbm, material_ref),
                (air_hbm, air_ref),
            ]
        )
    ]
    for load in loads:
        load.start()
    corner_np, column_np = element_keys()
    last = ELEMS // LANES

    def column_tile(ref, c, k):
        start = ELEMS - LANES if k == last else LANES * k
        return ref[c : c + 1, start : start + LANES]

    loads[0].wait()
    loads[3].wait()
    pieces, kinds = [], []
    for j in range(NH // SUBS):
        h = iota((SUBS, LANES), 0) + SUBS * j
        lane = iota((SUBS, LANES), 1)
        t = lane >> 5
        w = lane & (NW - 1)
        corner = (
            jnp.where(t == NT - 1, 4, 0) + jnp.where(h == NH - 1, 2, 0) + jnp.where(w == NW - 1, 1, 0)
        )
        column = (
            jnp.minimum(t, ET - 1) * (EH * EW)
            + jnp.minimum(h, EH - 1) * EW
            + jnp.minimum(w, EW - 1)
        )
        tile = column >> 7
        low = jnp.where(tile == last, column - (ELEMS - LANES), column & (LANES - 1))
        key = tile * 8 + corner
        rows = slice(SUBS * j, SUBS * (j + 1))
        wanted = sorted(set((column_np[rows] // LANES * 8 + corner_np[rows]).reshape(-1).tolist()))
        out = jnp.zeros((SUBS, LANES), jnp.int32)
        for code in wanted:
            c, k = code % 8, code // 8
            out = jnp.where(key == code, lane_pick(column_tile(conn_ref, c, k), low), out)
        pieces.append(out)
        kind = jnp.full((SUBS, LANES), -1, jnp.int32)
        for k in sorted({code // 8 for code in wanted if code % 8 == 0}):
            row = column_tile(material_ref, 0, k)
            kind = jnp.where((corner == 0) & (tile == k), lane_pick(row, low), kind)
        kinds.append(kind)
    nodes = jnp.concatenate(pieces, axis=0)
    nodes_ref[...] = nodes
    loads[1].wait()
    loads[2].wait()
    diag = look_up(lambda r: diag_ref[r : r + 1], ROWS, nodes)
    source = look_up(lambda r: source_ref[r : r + 1], ROWS, nodes)
    kind = jnp.concatenate(kinds, axis=0).astype(jnp.float32) + 1.0
    for ref in (even_ref, odd_ref):
        ref[0:ROWS] = diag
        ref[ROWS : 2 * ROWS] = source
        ref[2 * ROWS : 3 * ROWS] = kind

    loads[4].wait()
    fields, cells_z, cells_y, cells_x = air_ref.shape
    x_up = (fx & 1) == 0
    lane = iota((cells_y, LANES), 1)
    lows, highs = [], []
    for f in range(fields):
        low = jnp.zeros((cells_y, LANES), jnp.float32)
        high = jnp.zeros((cells_y, LANES), jnp.float32)
        for z in range(cells_z):
            x = pltpu.roll(air_ref[f, z], z + 1, 1)
            high = jnp.where(lane == z, x, high)
            low = jnp.where(lane == z + 1, x, low)
        lows.append(low)
        highs.append(high)
    low = pltpu.roll(jnp.concatenate(lows, axis=0), LANES - 1, 1)
    high = jnp.concatenate(highs, axis=0)
    even_ref[3 * ROWS :] = jnp.where(x_up, high, low).T[:cells_z]
    odd_ref[3 * ROWS :] = jnp.where(x_up, low, high).T[:cells_z]


def band_kernel(tiles_x, wide, *refs):
    parts, (rows_ref, z_even, z_odd) = refs[:tiles_x], refs[tiles_x : tiles_x + 3]
    even_ref, odd_ref, both_ref, held = refs[-4:]
    both_ref[BAND_ROWS : BAND_ROWS + rows_ref.shape[0], :LANES] = rows_ref[...]
    fields, cells_y = z_even.shape[:2]
    for f in range(fields):
        span = slice(BAND_ROWS + f * cells_y, BAND_ROWS + (f + 1) * cells_y)
        even_ref[span, :LANES] = z_even[f]
        odd_ref[span, :LANES] = z_odd[f]
    fx = lax.axis_index("fx")
    for k, part in enumerate(parts):
        held[fx ^ k] = part[0 : 3 * ROWS]
    lane = iota((NH, wide), 1)
    at = 0
    for field in range(3):
        for t in range(NT if field < 2 else ET):
            total = None
            for f in range(tiles_x):
                x = held[f, field * ROWS : (field + 1) * ROWS]
                if wide > LANES:
                    x = jnp.concatenate([x, jnp.zeros((NH, wide - LANES), jnp.float32)], axis=1)
                shift = (EW * f - NW * t) % wide
                if shift:
                    x = pltpu.roll(x, shift, 1)
                x = jnp.where((lane >= EW * f) & (lane < EW * f + NW), x, 0.0)
                total = x if total is None else total + x
            for ref in (even_ref, odd_ref, both_ref):
                ref[at : at + NH] = total
            at += NH


def air_kernel(tiles_x, tiles_y, others, air_ref, *refs):
    refs = list(refs)
    y_even = refs.pop(0)
    y_odd = refs.pop(0) if tiles_y > 2 else None
    x_even = refs.pop(0)
    x_odds = [(m, refs.pop(0)) for m in odd_masks(tiles_x)]
    refs = refs[others:]
    next_hbm, edge_ref, gain_ref, ends_ref, weight_ref, west_ref, east_ref, next_ref, sem = refs
    fx, fy = lax.axis_index("fx"), lax.axis_index("fy")
    fields, cells_z, cells_y, cells_x = air_ref.shape
    x_up = (fx & 1) == 0
    y_up = (fy & 1) == 0
    even = x_even[3 * ROWS :]
    odd = jnp.zeros_like(even)
    partner = jnp.where(x_up, fx - 1, fx + 1)
    for m, ref in x_odds:
        odd = jnp.where((fx ^ partner) == m, ref[3 * ROWS :], odd)
    pad = jnp.zeros((LANES - cells_z, LANES), jnp.float32)
    west_ref[...] = jnp.concatenate([jnp.where(x_up, odd, even), pad], axis=0).T
    east_ref[...] = jnp.concatenate([jnp.where(x_up, even, odd), pad], axis=0).T
    row = iota((cells_y, LANES), 0)
    lane = iota((cells_y, LANES), 1)
    half = 0.5 * time_step
    mix = time_step * viscosity

    def layer(z, below, above):
        u, v, w = air_ref[1, z], air_ref[2, z], air_ref[3, z]
        hu, hv, hw = half * u, half * v, half * w
        gain_ref[pl.ds(z, 1), :] = (mix + hv[0:1]) * jnp.where(fy == 0, 1.0, 0.0)
        for f in range(fields):
            x = air_ref[f, z]
            span = slice(f * cells_y, (f + 1) * cells_y)
            west = jnp.where(
                lane == 0,
                pltpu.roll(west_ref[span], (LANES - z) % LANES, 1),
                pltpu.roll(x, 1, 1),
            )
            east = jnp.where(
                lane == LANES - 1,
                pltpu.roll(east_ref[span], LANES - 1 - z, 1),
                pltpu.roll(x, LANES - 1, 1),
            )
            y_e = y_even[f, pl.ds(z, 1), :]
            y_o = y_odd[f, pl.ds(z, 1), :] if y_odd is not None else jnp.zeros_like(y_e)
            south_ghost = jnp.where(y_up, y_o, y_e)
            north_ghost = jnp.where(y_up, y_e, y_o)
            south = jnp.where(row == 0, south_ghost, pltpu.roll(x, 1, 0))
            north = jnp.where(row == cells_y - 1, north_ghost, pltpu.roll(x, cells_y - 1, 0))
            lower, upper = below(f), above(f)
            out = (
                (1.0 - 6.0 * mix) * x
                + mix * (east + west + north + south + upper + lower)
                + hu * (west - east)
                + hv * (south - north)
                + hw * (lower - upper)
            )
            next_ref[f, z] = out
            if f == 0:
                edge_ref[z] = out[:SUBS]

    def outside(f):
        return jnp.zeros((cells_y, LANES), jnp.float32)

    steps = 4
    depth = cells_z // steps
    for step in range(steps):
        start, stop = step * depth, (step + 1) * depth
        if start == 0:
            layer(0, outside, lambda f: air_ref[f, 1])

        @pl.loop(max(start, 1), min(stop, cells_z - 1))
        def _(z):
            layer(z, lambda f: air_ref[f, z - 1], lambda f: air_ref[f, z + 1])

        if stop == cells_z:
            layer(cells_z - 1, lambda f: air_ref[f, cells_z - 2], outside)
        pltpu.make_async_copy(
            next_ref.at[:, start:stop], next_hbm.at[:, start:stop], sem
        ).start()
    for i, z in enumerate((0, cells_z - 1)):
        hw = half * air_ref[3, z]
        weight_ref[i] = mix - hw if i else mix + hw
        ends_ref[i] = next_ref[:, z]
    pltpu.make_async_copy(next_ref, next_hbm, sem).wait()


def place_kernel(
    nodes_ref, iface_ref, air_ref, place_ref, rows_ref, y_even, y_odd, z_even, z_odd
):
    sec, fy = lax.axis_index("sec"), lax.axis_index("fy")
    fields, cells_z, cells_y, cells_x = air_ref.shape
    z_up = (sec & 1) == 0
    z_even[...] = air_ref[:, jnp.where(z_up, cells_z - 1, 0)]
    z_odd[...] = air_ref[:, jnp.where(z_up, 0, cells_z - 1)]
    y_up = (fy & 1) == 0
    for f in range(fields):
        first = air_ref[f, :, 0, :]
        last = air_ref[f, :, cells_y - 1, :]
        y_even[f] = jnp.where(y_up, last, first)
        y_odd[f] = jnp.where(y_up, first, last)
    nodes = nodes_ref[...]
    at_row = iota(nodes.shape, 0).astype(jnp.float32)
    at_lane = iota(nodes.shape, 1).astype(jnp.float32)
    high, low = spread(nodes, [at_row, at_lane])
    place = high * LANES + low
    place_ref[...] = place.astype(jnp.int32)
    count = iface_ref.shape[-1] // LANES
    iface = jnp.concatenate(
        [iface_ref[0:1, LANES * r : LANES * (r + 1)] for r in range(count)], axis=0
    )
    rows_ref[...] = look_up(lambda r: place[r : r + 1], ROWS, iface)


def face_kernel(tiles_y, face_ref, *refs):
    parts, wall_ref, held = refs[:tiles_y], refs[tiles_y], refs[tiles_y + 1]
    fy = lax.axis_index("fy")
    for k, part in enumerate(parts):
        count = held.shape[1]
        rows = part[BAND_ROWS : BAND_ROWS + count, :LANES]
        held[fy ^ k] = rows + (fy ^ k).astype(jnp.float32) * (ROWS * LANES)
    rows = jnp.concatenate([held[j] for j in range(tiles_y)], axis=0)
    row = rows.astype(jnp.int32)
    high, low = spread(
        face_ref[...],
        [(row >> 7).astype(jnp.float32), (row & (LANES - 1)).astype(jnp.float32)],
    )
    wall_ref[...] = (high * LANES + low).astype(jnp.int32)


def solve_kernel(
    tiles_s, tiles_x, tiles_y, wide, material_count,
    conduct_ref, capacity_ref, place_ref, wall_ref, edge_ref, gain_ref, ends_ref, weight_ref, air_ref,
    *refs,
):
    bands = tiles_s * tiles_y
    parts = refs[:bands]
    solid_ref, next_ref = refs[bands : bands + 2]
    (held, elem, side, main, inv, res, dirn, image, sol, table, last_table, edge, solid, ends, sem) = refs[
        bands + 2 :
    ]
    sec, fx, fy = (lax.axis_index(axis) for axis in ("sec", "fx", "fy"))
    z_up = (sec & 1) == 0
    fields, cells_z, cells_y = air_ref.shape[:3]
    z_odds = [(m, parts[m]) for m in odd_masks(tiles_s)]
    across = sec ^ jnp.where(z_up, sec - 1, sec + 1)
    outer = [
        pltpu.make_async_copy(ends.at[i], next_ref.at[:, z], sem.at[2 + i])
        for i, z in enumerate((0, cells_z - 1))
    ]
    lane_tiles = [slice(i, i + LANES) for i in range(0, wide, LANES)]
    small = bands * wide <= SUBS * LANES

    def take(part, band):
        count = BAND_ROWS if small else SUBS

        def body(n, carry):
            for i, cut in enumerate(lane_tiles):
                held[i, pl.ds(band + n * (count * bands), count, stride=bands), :] = part[
                    pl.ds(n * count, count), cut
                ]
            return carry

        if small:
            body(0, 0)
        else:
            lax.fori_loop(0, BAND_ROWS // count, body, 0)

    @pl.when(fy >= 0)
    def _():
        for i, copy in enumerate(outer):
            for f in range(fields):
                span = slice(BAND_ROWS + f * cells_y, BAND_ROWS + (f + 1) * cells_y)
                even = parts[1][span, :LANES]
                odd = jnp.zeros_like(even)
                for m, part in z_odds:
                    odd = jnp.where(across == m, part[span, :LANES], odd)
                here, there = (odd, even) if i == 0 else (even, odd)
                ends[i, f] = ends_ref[i, f] + weight_ref[i] * jnp.where(z_up, here, there)
            copy.start()

    @pl.when(fy >= 0)
    def _():
        for j in range(tiles_y):
            for k in range(tiles_s):
                band = (sec ^ k) * tiles_y + (fy ^ j)
                take(parts[j * tiles_s + k], band)

    def loop(start, stop, body, carry):
        if not small:
            return lax.fori_loop(start, stop, body, carry)
        for h in range(start, stop):
            carry = body(h, carry)
        return carry

    def span_of(r):
        return pl.ds(r * bands if isinstance(r, int) else pl.multiple_of(r * bands, bands), bands)

    def join(tiles):
        return tiles[0] if len(tiles) == 1 else jnp.concatenate(tiles, axis=1)

    def row_of(ref, r):
        return join([ref[i, span_of(r), :] for i in range(len(lane_tiles))])

    def put(ref, r, x):
        for i, cut in enumerate(lane_tiles):
            ref[i, span_of(r), :] = x[:, cut]

    lane = iota((bands, wide), 1)
    band = iota((bands, wide), 0)
    used = lane < EW * tiles_x + 1

    def right(x):
        return pltpu.roll(x, wide - 1, 1)

    def left(x):
        return pltpu.roll(x, 1, 1)

    def plus(*terms):
        terms = [x for x in terms if x is not None]
        total = terms[0] if terms else None
        for x in terms[1:]:
            total = total + x
        return total

    def seam(low, high):
        below = jnp.where(band > 0, pltpu.roll(high, 1, 0), 0.0)
        above = jnp.where(band < bands - 1, pltpu.roll(low, bands - 1, 0), 0.0)
        return low + below, high + above

    def total_of(parts):
        x = plus(*parts)
        return jnp.sum(jnp.sum(x, axis=0, keepdims=True), axis=1, keepdims=True)

    def first_row(ref, x, n):
        return seam(x, row_of(ref, n + NH - 1))[0]

    def last_row(ref, x, n):
        return seam(row_of(ref, n - NH + 1), x)[1]

    def once(x):
        return jnp.where(band > 0, 0.0, x)

    zero = jnp.zeros((bands, wide), jnp.float32)

    @pl.when(fy >= 0)
    def _():
        def prepare(h, before):
            now = []
            for t in range(ET):
                kind = row_of(held, 2 * FIELD_ROWS + t * NH + h)
                x = jnp.zeros_like(kind)
                s = jnp.zeros_like(kind)
                for m in range(material_count):
                    x = jnp.where(kind == m + 1.0, conduct_ref[m] * (1.0 / 12.0), x)
                    s = jnp.where(kind == m + 1.0, capacity_ref[m] * 0.125, s)
                put(elem, t * NH + h, x)
                now += [x, 5.0 * x + s]
            both = [a + b for a, b in zip(now, before)]
            for t in range(NT):
                if t < ET:
                    x = both[2 * t]
                    put(side, t * NH + h, x + left(x))
                x = plus(both[2 * t + 1] if t < ET else None, both[2 * t - 1] if t else None)
                put(main, t * NH + h, x + left(x))
            return tuple(now)

        loop(0, NH, prepare, (zero,) * (2 * ET))

    def begin(h, acc, fix=None):
        out = []
        for t in range(NT):
            n = t * NH + h
            d, r = row_of(held, n), row_of(held, FIELD_ROWS + n)
            if fix is not None:
                d, r = fix(held, d, n), fix(held, r, FIELD_ROWS + n)
            v = jnp.where(used, 1.0 / d, 0.0)
            z = r * v
            put(inv, n, v)
            put(res, n, r)
            put(dirn, n, z)
            out.append(acc[t] + (once(r * z) if fix is first_row else r * z))
        return tuple(out)

    acc = begin(0, (zero,) * NT, first_row)
    acc = begin(NH - 1, acc, last_row)
    acc = loop(1, NH - 1, begin, acc)
    gamma = total_of(acc)

    def operate(iteration, beta, step_len):
        last = iteration + 1 == ITERS

        def fetch(h):
            p, y = [], []
            for t in range(NT):
                n = t * NH + h
                x = row_of(dirn, n)
                if beta is not None:
                    put(sol, n, plus(step_len * x, row_of(sol, n) if iteration > 1 else None))
                    x = row_of(res, n) * row_of(inv, n) + beta * x
                    put(dirn, n, x)
                p.append(x)
                y.append(right(x))
            return p, y

        def finish(h, p, diag_now, cross_now, on_diag, on_cross, acc):
            out_acc = []
            for t in range(NT):
                n = t * NH + h
                out = row_of(main, n) * p[t]
                if t < ET:
                    out = out + row_of(side, n) * p[t + 1]
                if t > 0:
                    out = out + row_of(side, n - NH) * p[t - 1]
                out = out - plus(
                    diag_now[t], on_cross[t], left(plus(cross_now[t], on_diag[t]))
                )
                if not last:
                    put(image, n, out)
                out_acc.append(acc[t] + p[t] * out)
            return out_acc

        def body(h, carry):
            p, y, on_diag, on_cross, acc = (carry[i * NT : (i + 1) * NT] for i in range(5))
            p_next, y_next = fetch(h + 1)
            diag = [p[t] + y_next[t] for t in range(NT)]
            cross = [y[t] + p_next[t] for t in range(NT)]
            layer = [a + b for a, b in zip(diag, cross)]
            x = [row_of(elem, t * NH + h) for t in range(ET)]
            diag_now, cross_now = [], []
            for t in range(NT):
                upper = x[t] if t < ET else None
                lower = x[t - 1] if t > 0 else None
                both = plus(upper, lower)
                other = plus(
                    upper * layer[t + 1] if t < ET else None,
                    lower * layer[t - 1] if t > 0 else None,
                )
                diag_now.append(other + both * diag[t])
                cross_now.append(other + both * cross[t])
            acc = finish(h, p, diag_now, cross_now, on_diag, on_cross, acc)
            return (*p_next, *y_next, *diag_now, *cross_now, *acc)

        p, y = fetch(0)
        carry = loop(0, EH, body, (*p, *y) + (zero,) * (3 * NT))
        p, y, on_diag, on_cross, acc = (carry[i * NT : (i + 1) * NT] for i in range(5))
        none = [None] * NT
        acc = finish(EH, p, none, none, on_diag, on_cross, acc)
        if last:
            for j in range(tiles_y):
                table[j] = pack(sol, j)
                last_table[j] = pack(dirn, j)
        return total_of(acc)

    spot = iota((NH, LANES), 1) >> 5

    def pack(ref, j):
        packed = None
        for t in range(NT):
            start = t * NH * bands + sec * tiles_y + j
            x = join(
                [ref[i, pl.ds(start, NH, stride=bands), :] for i in range(len(lane_tiles))]
            )
            x = pltpu.roll(x, (NW * t - EW * fx + tiles_x * wide) % wide, 1)[:, :LANES]
            packed = x if packed is None else jnp.where(spot == t, x, packed)
        return packed

    beta = step_len = None
    for iteration in range(ITERS):
        step_len = gamma / operate(iteration, beta, step_len)
        if iteration + 1 == ITERS:
            break

        def update(h, acc, fix=None, step_len=step_len):
            out = []
            for t in range(NT):
                n = t * NH + h
                q = row_of(image, n)
                if fix is not None:
                    q = fix(image, q, n)
                r = row_of(res, n) - step_len * q
                put(res, n, r)
                part = r * r * row_of(inv, n)
                out.append(acc[t] + (once(part) if fix is first_row else part))
            return tuple(out)

        acc = update(0, (zero,) * NT, first_row)
        acc = update(NH - 1, acc, last_row)
        gamma_next = total_of(loop(1, NH - 1, update, acc))
        beta = gamma_next / gamma
        gamma = gamma_next

    for j in range(tiles_y):
        table[j] = table[j] + step_len * last_table[j]
    last_table[0] = table[fy]
    first = pltpu.make_async_copy(solid, solid_ref, sem.at[0])
    second = pltpu.make_async_copy(edge, next_ref.at[0, :, 0:SUBS, :], sem.at[1])

    @pl.when(fy >= 0)
    def _():
        solid[...] = look_up(lambda r: last_table[0, r : r + 1], ROWS, place_ref[...])
        first.start()

    for copy in outer:
        copy.wait()

    @pl.when(fy == 0)
    def _():
        extra = look_up(
            lambda r: table[r // ROWS, r % ROWS : r % ROWS + 1], tiles_y * ROWS, wall_ref[...]
        )
        extra = extra * gain_ref[...]
        top = iota((SUBS, LANES), 0) == 0
        for z in range(cells_z):
            base = ends[z // (cells_z - 1), 0, :SUBS] if z in (0, cells_z - 1) else edge_ref[z]
            edge[z] = base + jnp.where(top, extra[z : z + 1], 0.0)
        second.start()
        second.wait()

    first.wait()


def odd_masks(count):
    return sorted({i ^ (i + 1) for i in range(1, count - 1, 2)})


def swap(x, axis, mask):
    count = lax.axis_size(axis)
    return lax.ppermute(x, axis, [(i, i ^ mask) for i in range(count)])


def pair_swap(x, axis, odd):
    count = lax.axis_size(axis)
    pairs = []
    for i in range(odd, count - 1, 2):
        pairs += [(i, i + 1), (i + 1, i)]
    return lax.ppermute(x, axis, pairs) if pairs else jnp.zeros_like(x)


def on_device(
    conn,
    material,
    side_nodes,
    rim_nodes,
    iface_node,
    face_of_row,
    conductivity,
    capacity,
    diag_part,
    heat_source,
    air_state,
):
    f32 = jnp.float32
    tiles_s, tiles_x, tiles_y = (lax.axis_size(axis) for axis in ("sec", "fx", "fy"))
    bands = tiles_s * tiles_y
    wide = -(-(EW * tiles_x + 1) // LANES) * LANES
    fields, cells_z, cells_y, cells_x = air_state.shape

    def call(kernel, args, specs, outs, out_specs, scratch=(), **more):
        held = list(args) + list(outs) + [s for s in scratch if hasattr(s, "shape")]
        need = sum(4 * int(np.prod(x.shape)) for x in held)
        return pl.pallas_call(
            kernel,
            in_specs=specs,
            out_specs=out_specs,
            out_shape=outs,
            scratch_shapes=list(scratch),
            compiler_params=pltpu.CompilerParams(vmem_limit_bytes=need + (6 << 20)),
            **more,
        )(*args)

    def cost(microseconds):
        return pl.CostEstimate(
            flops=0, bytes_accessed=int(3.7e6 * microseconds), transcendentals=0
        )

    def shape(*dims):
        return jax.ShapeDtypeStruct(dims, f32)

    def ints(*dims):
        return jax.ShapeDtypeStruct(dims, jnp.int32)

    even, odd, nodes, air = call(
        stage_kernel,
        [
            pltpu.with_memory_space_constraint(x, pltpu.HBM)
            for x in (
                conn.reshape(conn.shape[-2:]),
                material.reshape(1, -1),
                diag_part.reshape(ROWS, LANES),
                heat_source.reshape(ROWS, LANES),
                air_state,
            )
        ],
        [HBM] * 5,
        [
            shape(3 * ROWS + cells_z, LANES),
            shape(3 * ROWS + cells_z, LANES),
            ints(ROWS, LANES),
            shape(*air_state.shape),
        ],
        [VMEM] * 4,
        [
            pltpu.VMEM(conn.shape[-2:], jnp.int32),
            pltpu.VMEM((1, material.shape[-1]), jnp.int32),
            pltpu.VMEM((ROWS, LANES), f32),
            pltpu.VMEM((ROWS, LANES), f32),
            pltpu.SemaphoreType.DMA((5,)),
        ],
    )
    odds = odd_masks(tiles_x)
    pays = [even] + [
        swap(odd if k in odds else even, "fx", k) for k in range(1, tiles_x)
    ]
    place, rows, y_even, y_odd, z_even, z_odd = call(
        place_kernel,
        [nodes, iface_node.reshape(1, -1), air],
        [VMEM] * 3,
        [ints(ROWS, LANES), shape(iface_node.shape[-1] // LANES, LANES)]
        + [shape(fields, cells_z, cells_x)] * 2
        + [shape(fields, cells_y, cells_x)] * 2,
        [VMEM] * 6,
        cost_estimate=cost(0.6),
    )

    y_ghosts = [pair_swap(y_even, "fy", 0)]
    if tiles_y > 2:
        y_ghosts.append(pair_swap(y_odd, "fy", 1))

    ghosts = list(y_ghosts)
    even, odd, both = call(
        lambda *refs: band_kernel(tiles_x, wide, *refs),
        pays + [rows, z_even, z_odd] + ghosts,
        [VMEM] * (tiles_x + 3) + [ANY] * len(ghosts),
        [shape(BAND_ROWS + fields * cells_y, wide)] * 2
        + [shape(BAND_ROWS + 2 * SUBS, wide)],
        [VMEM] * 3,
        [pltpu.VMEM((tiles_x, 3 * ROWS, LANES), f32)],
        cost_estimate=cost(0.3),
    )
    z_odds = odd_masks(tiles_s)
    own_bands = [even] + [
        swap(odd if k in z_odds else even, "sec", k) for k in range(1, tiles_s)
    ]
    boths = [both] + [swap(both, "fy", j) for j in range(1, tiles_y)]
    wall = call(
        lambda *refs: face_kernel(tiles_y, *refs),
        [face_of_row.reshape(-1, LANES)] + boths,
        [VMEM] * (1 + tiles_y),
        [ints(cells_z, LANES)],
        [VMEM],
        [pltpu.VMEM((tiles_y,) + rows.shape, f32)],
        cost_estimate=cost(0.5),
    )[0]

    ghosts += [pays[1]] + [pays[m] for m in odds]
    others = [wall] + [pays[k] for k in range(2, tiles_x) if k not in odds]
    air_next, edge, gain, ends, weight = call(
        lambda *refs: air_kernel(tiles_x, tiles_y, len(others), *refs),
        [air] + ghosts + others,
        [VMEM] * (1 + len(ghosts)) + [ANY] * len(others),
        [
            shape(*air_state.shape),
            shape(cells_z, SUBS, LANES),
            shape(cells_z, LANES),
            shape(2, fields, cells_y, cells_x),
            shape(2, cells_y, cells_x),
        ],
        [ANY] + [VMEM] * 4,
        [pltpu.VMEM((LANES, LANES), f32)] * 2
        + [pltpu.VMEM(air_state.shape, f32), pltpu.SemaphoreType.DMA],
        cost_estimate=cost(4.0),
    )

    marks = [edge, gain, ends]
    for k in range(1, tiles_s):
        i = (k - 1) % len(marks)
        own_bands[k], marks[i] = lax.optimization_barrier((own_bands[k], marks[i]))
    edge, gain, ends = marks
    all_bands = list(own_bands)
    for j in range(1, tiles_y):
        all_bands += [boths[j]] + [swap(b, "fy", j) for b in own_bands[1:]]

    grid = (wide // LANES, NT * NH * bands, LANES)
    solid, air_next = call(
        lambda *refs: solve_kernel(
            tiles_s, tiles_x, tiles_y, wide, conductivity.shape[0], *refs
        ),
        [conductivity, capacity, place, wall, edge, gain, ends, weight, air_next]
        + all_bands,
        [SMEM] * 2 + [VMEM] * 6 + [ANY] + [VMEM] * bands,
        [shape(ROWS, LANES), shape(*air_state.shape)],
        [ANY, ANY],
        [pltpu.VMEM((wide // LANES, BAND_ROWS * bands, LANES), f32)]
        + [pltpu.VMEM(grid, f32)] * 8
        + [
            pltpu.VMEM((tiles_y, ROWS, LANES), f32),
            pltpu.VMEM((tiles_y, ROWS, LANES), f32),
            pltpu.VMEM((cells_z, SUBS, LANES), f32),
            pltpu.VMEM((ROWS, LANES), f32),
            pltpu.VMEM((2, fields, cells_y, cells_x), f32),
            pltpu.SemaphoreType.DMA((4,)),
        ],
        input_output_aliases={8: 1},
    )
    return solid.reshape(diag_part.shape), air_next


def solution(mesh):
    return jax.shard_map(
        on_device,
        mesh=mesh,
        in_specs=(
            P("sec", "fx", "fy", None, None),
            P("sec", "fx", "fy", None),
            P("sec", "fx", "fy", None, None),
            P("sec", "fx", "fy", None, None),
            P("sec", "fx", "fy", None),
            P("sec", "fx", None),
            P(),
            P(),
            P("sec", "fx", "fy", None),
            P("sec", "fx", "fy", None),
            P(None, "sec", "fy", "fx"),
        ),
        out_specs=(P("sec", "fx", "fy", None), P(None, "sec", "fy", "fx")),
        check_vma=False,
    )
```

```python
import jax
import jax.numpy as jnp
import numpy as np
from jax import lax
from jax.experimental import pallas as pl
from jax.experimental.pallas import tpu as pltpu
from jax.sharding import PartitionSpec as P

NW = 32
NH = 24
NT = 4
ITERS = 4
LANES = 128
SUBS = 8

time_step = 0.2
viscosity = 0.75

VMEM = pl.BlockSpec(memory_space=pltpu.VMEM)
SMEM = pl.BlockSpec(memory_space=pltpu.SMEM)
ANY = pl.BlockSpec(memory_space=pl.ANY)
HBM = pl.BlockSpec(memory_space=pltpu.HBM)

EW = NW - 1
EH = NH - 1
ET = NT - 1
ELEMS = ET * EH * EW
ROWS = NT * NH * NW // LANES
FIELD_ROWS = NT * NH
BAND_ROWS = 2 * FIELD_ROWS + ET * NH


def iota(shape, dim):
    return lax.broadcasted_iota(jnp.int32, shape, dim)


def lane_pick(row, idx):
    return jnp.take_along_axis(
        jnp.broadcast_to(row, idx.shape), idx, axis=1, mode="promise_in_bounds"
    )


def look_up(load, count, place):
    outs = []
    for start in range(0, place.shape[0], SUBS):
        part = place[start : start + SUBS]
        high = part >> 7
        low = part & (LANES - 1)
        out = None
        for r in range(count):
            got = lane_pick(load(r), low)
            out = got if out is None else jnp.where(high == r, got, out)
        outs.append(out)
    return jnp.concatenate(outs, axis=0) if len(outs) > 1 else outs[0]


def spread(idx, values):
    count = idx.shape[0]
    acc = None
    group = 4
    for start in range(0, count, group):
        left, right = [], []
        for r in range(start, start + group):
            row = idx[r : r + 1]
            hot_high = iota((count, LANES), 0) == (row >> 7)
            hot_low = iota((LANES, LANES), 0) == (row & (LANES - 1))
            left.append(
                jnp.concatenate(
                    [jnp.where(hot_high, v[r : r + 1], 0.0) for v in values], axis=0
                ).astype(jnp.bfloat16)
            )
            right.append(jnp.where(hot_low, 1.0, 0.0).astype(jnp.bfloat16))
        part = lax.dot_general(
            jnp.concatenate(left, axis=1),
            jnp.concatenate(right, axis=1),
            (((1,), (1,)), ((), ())),
            preferred_element_type=jnp.float32,
        )
        acc = part if acc is None else acc + part
    return [acc[i * count : (i + 1) * count] for i in range(len(values))]


def element_keys():
    h = np.arange(NH)[:, None]
    lane = np.arange(LANES)[None, :]
    t, w = lane // NW, lane % NW
    corner = 4 * (t == NT - 1) + 2 * (h == NH - 1) + (w == NW - 1)
    column = np.minimum(t, ET - 1) * EH * EW + np.minimum(h, EH - 1) * EW + np.minimum(w, EW - 1)
    return corner, column


def stage_kernel(
    conn_hbm, material_hbm, diag_hbm, source_hbm, air_hbm,
    even_ref, odd_ref, nodes_ref, air_ref,
    conn_ref, material_ref, diag_ref, source_ref, sem,
):
    fx = lax.axis_index("fx")
    loads = [
        pltpu.make_async_copy(a, b, sem.at[i])
        for i, (a, b) in enumerate(
            [
                (conn_hbm, conn_ref),
                (diag_hbm, diag_ref),
                (source_hbm, source_ref),
                (material_hbm, material_ref),
                (air_hbm, air_ref),
            ]
        )
    ]
    for load in loads:
        load.start()
    corner_np, column_np = element_keys()
    last = ELEMS // LANES

    def column_tile(ref, c, k):
        start = ELEMS - LANES if k == last else LANES * k
        return ref[c : c + 1, start : start + LANES]

    loads[0].wait()
    loads[3].wait()
    pieces, kinds = [], []
    for j in range(NH // SUBS):
        h = iota((SUBS, LANES), 0) + SUBS * j
        lane = iota((SUBS, LANES), 1)
        t = lane >> 5
        w = lane & (NW - 1)
        corner = (
            jnp.where(t == NT - 1, 4, 0) + jnp.where(h == NH - 1, 2, 0) + jnp.where(w == NW - 1, 1, 0)
        )
        column = (
            jnp.minimum(t, ET - 1) * (EH * EW)
            + jnp.minimum(h, EH - 1) * EW
            + jnp.minimum(w, EW - 1)
        )
        tile = column >> 7
        low = jnp.where(tile == last, column - (ELEMS - LANES), column & (LANES - 1))
        key = tile * 8 + corner
        rows = slice(SUBS * j, SUBS * (j + 1))
        wanted = sorted(set((column_np[rows] // LANES * 8 + corner_np[rows]).reshape(-1).tolist()))
        out = jnp.zeros((SUBS, LANES), jnp.int32)
        for code in wanted:
            c, k = code % 8, code // 8
            out = jnp.where(key == code, lane_pick(column_tile(conn_ref, c, k), low), out)
        pieces.append(out)
        kind = jnp.full((SUBS, LANES), -1, jnp.int32)
        for k in sorted({code // 8 for code in wanted if code % 8 == 0}):
            row = column_tile(material_ref, 0, k)
            kind = jnp.where((corner == 0) & (tile == k), lane_pick(row, low), kind)
        kinds.append(kind)
    nodes = jnp.concatenate(pieces, axis=0)
    nodes_ref[...] = nodes
    loads[1].wait()
    loads[2].wait()
    diag = look_up(lambda r: diag_ref[r : r + 1], ROWS, nodes)
    source = look_up(lambda r: source_ref[r : r + 1], ROWS, nodes)
    kind = jnp.concatenate(kinds, axis=0).astype(jnp.float32) + 1.0
    for ref in (even_ref, odd_ref):
        ref[0:ROWS] = diag
        ref[ROWS : 2 * ROWS] = source
        ref[2 * ROWS : 3 * ROWS] = kind

    loads[4].wait()
    fields, cells_z, cells_y, cells_x = air_ref.shape
    x_up = (fx & 1) == 0
    lane = iota((cells_y, LANES), 1)
    lows, highs = [], []
    for f in range(fields):
        low = jnp.zeros((cells_y, LANES), jnp.float32)
        high = jnp.zeros((cells_y, LANES), jnp.float32)
        for z in range(cells_z):
            x = pltpu.roll(air_ref[f, z], z + 1, 1)
            high = jnp.where(lane == z, x, high)
            low = jnp.where(lane == z + 1, x, low)
        lows.append(low)
        highs.append(high)
    low = pltpu.roll(jnp.concatenate(lows, axis=0), LANES - 1, 1)
    high = jnp.concatenate(highs, axis=0)
    even_ref[3 * ROWS :] = jnp.where(x_up, high, low).T[:cells_z]
    odd_ref[3 * ROWS :] = jnp.where(x_up, low, high).T[:cells_z]


def band_kernel(tiles_x, wide, *refs):
    parts, (rows_ref, z_even, z_odd) = refs[:tiles_x], refs[tiles_x : tiles_x + 3]
    even_ref, odd_ref, both_ref, held = refs[-4:]
    both_ref[BAND_ROWS : BAND_ROWS + rows_ref.shape[0], :LANES] = rows_ref[...]
    fields, cells_y = z_even.shape[:2]
    for f in range(fields):
        span = slice(BAND_ROWS + f * cells_y, BAND_ROWS + (f + 1) * cells_y)
        even_ref[span, :LANES] = z_even[f]
        odd_ref[span, :LANES] = z_odd[f]
    fx = lax.axis_index("fx")
    for k, part in enumerate(parts):
        held[fx ^ k] = part[0 : 3 * ROWS]
    lane = iota((NH, wide), 1)
    at = 0
    for field in range(3):
        for t in range(NT if field < 2 else ET):
            total = None
            for f in range(tiles_x):
                x = held[f, field * ROWS : (field + 1) * ROWS]
                if wide > LANES:
                    x = jnp.concatenate([x, jnp.zeros((NH, wide - LANES), jnp.float32)], axis=1)
                shift = (EW * f - NW * t) % wide
                if shift:
                    x = pltpu.roll(x, shift, 1)
                x = jnp.where((lane >= EW * f) & (lane < EW * f + NW), x, 0.0)
                total = x if total is None else total + x
            for ref in (even_ref, odd_ref, both_ref):
                ref[at : at + NH] = total
            at += NH


def air_kernel(tiles_x, tiles_y, others, air_ref, *refs):
    refs = list(refs)
    y_even = refs.pop(0)
    y_odd = refs.pop(0) if tiles_y > 2 else None
    x_even = refs.pop(0)
    x_odds = [(m, refs.pop(0)) for m in odd_masks(tiles_x)]
    refs = refs[others:]
    next_hbm, edge_ref, gain_ref, ends_ref, weight_ref, west_ref, east_ref, next_ref, sem = refs
    fx, fy = lax.axis_index("fx"), lax.axis_index("fy")
    fields, cells_z, cells_y, cells_x = air_ref.shape
    x_up = (fx & 1) == 0
    y_up = (fy & 1) == 0
    even = x_even[3 * ROWS :]
    odd = jnp.zeros_like(even)
    partner = jnp.where(x_up, fx - 1, fx + 1)
    for m, ref in x_odds:
        odd = jnp.where((fx ^ partner) == m, ref[3 * ROWS :], odd)
    pad = jnp.zeros((LANES - cells_z, LANES), jnp.float32)
    west_ref[...] = jnp.concatenate([jnp.where(x_up, odd, even), pad], axis=0).T
    east_ref[...] = jnp.concatenate([jnp.where(x_up, even, odd), pad], axis=0).T
    row = iota((cells_y, LANES), 0)
    lane = iota((cells_y, LANES), 1)
    half = 0.5 * time_step
    mix = time_step * viscosity

    def layer(z, below, above):
        u, v, w = air_ref[1, z], air_ref[2, z], air_ref[3, z]
        hu, hv, hw = half * u, half * v, half * w
        gain_ref[pl.ds(z, 1), :] = (mix + hv[0:1]) * jnp.where(fy == 0, 1.0, 0.0)
        for f in range(fields):
            x = air_ref[f, z]
            span = slice(f * cells_y, (f + 1) * cells_y)
            west = jnp.where(
                lane == 0,
                pltpu.roll(west_ref[span], (LANES - z) % LANES, 1),
                pltpu.roll(x, 1, 1),
            )
            east = jnp.where(
                lane == LANES - 1,
                pltpu.roll(east_ref[span], LANES - 1 - z, 1),
                pltpu.roll(x, LANES - 1, 1),
            )
            y_e = y_even[f, pl.ds(z, 1), :]
            y_o = y_odd[f, pl.ds(z, 1), :] if y_odd is not None else jnp.zeros_like(y_e)
            south_ghost = jnp.where(y_up, y_o, y_e)
            north_ghost = jnp.where(y_up, y_e, y_o)
            south = jnp.where(row == 0, south_ghost, pltpu.roll(x, 1, 0))
            north = jnp.where(row == cells_y - 1, north_ghost, pltpu.roll(x, cells_y - 1, 0))
            lower, upper = below(f), above(f)
            out = (
                (1.0 - 6.0 * mix) * x
                + mix * (east + west + north + south + upper + lower)
                + hu * (west - east)
                + hv * (south - north)
                + hw * (lower - upper)
            )
            next_ref[f, z] = out
            if f == 0:
                edge_ref[z] = out[:SUBS]

    def outside(f):
        return jnp.zeros((cells_y, LANES), jnp.float32)

    steps = 4
    depth = cells_z // steps
    for step in range(steps):
        start, stop = step * depth, (step + 1) * depth
        if start == 0:
            layer(0, outside, lambda f: air_ref[f, 1])

        @pl.loop(max(start, 1), min(stop, cells_z - 1), unroll=True)
        def _(z):
            layer(z, lambda f: air_ref[f, z - 1], lambda f: air_ref[f, z + 1])

        if stop == cells_z:
            layer(cells_z - 1, lambda f: air_ref[f, cells_z - 2], outside)
        pltpu.make_async_copy(
            next_ref.at[:, start:stop], next_hbm.at[:, start:stop], sem
        ).start()
    for i, z in enumerate((0, cells_z - 1)):
        hw = half * air_ref[3, z]
        weight_ref[i] = mix - hw if i else mix + hw
        ends_ref[i] = next_ref[:, z]
    pltpu.make_async_copy(next_ref, next_hbm, sem).wait()


def place_kernel(
    nodes_ref, iface_ref, air_ref, place_ref, rows_ref, y_even, y_odd, z_even, z_odd
):
    sec, fy = lax.axis_index("sec"), lax.axis_index("fy")
    fields, cells_z, cells_y, cells_x = air_ref.shape
    z_up = (sec & 1) == 0
    z_even[...] = air_ref[:, jnp.where(z_up, cells_z - 1, 0)]
    z_odd[...] = air_ref[:, jnp.where(z_up, 0, cells_z - 1)]
    y_up = (fy & 1) == 0
    for f in range(fields):
        first = air_ref[f, :, 0, :]
        last = air_ref[f, :, cells_y - 1, :]
        y_even[f] = jnp.where(y_up, last, first)
        y_odd[f] = jnp.where(y_up, first, last)
    nodes = nodes_ref[...]
    at_row = iota(nodes.shape, 0).astype(jnp.float32)
    at_lane = iota(nodes.shape, 1).astype(jnp.float32)
    high, low = spread(nodes, [at_row, at_lane])
    place = high * LANES + low
    place_ref[...] = place.astype(jnp.int32)
    count = iface_ref.shape[-1] // LANES
    iface = jnp.concatenate(
        [iface_ref[0:1, LANES * r : LANES * (r + 1)] for r in range(count)], axis=0
    )
    rows_ref[...] = look_up(lambda r: place[r : r + 1], ROWS, iface)


def face_kernel(tiles_y, face_ref, *refs):
    parts, wall_ref, held = refs[:tiles_y], refs[tiles_y], refs[tiles_y + 1]
    fy = lax.axis_index("fy")
    for k, part in enumerate(parts):
        count = held.shape[1]
        rows = part[BAND_ROWS : BAND_ROWS + count, :LANES]
        held[fy ^ k] = rows + (fy ^ k).astype(jnp.float32) * (ROWS * LANES)
    rows = jnp.concatenate([held[j] for j in range(tiles_y)], axis=0)
    row = rows.astype(jnp.int32)
    high, low = spread(
        face_ref[...],
        [(row >> 7).astype(jnp.float32), (row & (LANES - 1)).astype(jnp.float32)],
    )
    wall_ref[...] = (high * LANES + low).astype(jnp.int32)


def solve_kernel(
    tiles_s, tiles_x, tiles_y, wide, material_count,
    conduct_ref, capacity_ref, place_ref, wall_ref, edge_ref, gain_ref, ends_ref, weight_ref, air_ref,
    *refs,
):
    bands = tiles_s * tiles_y
    parts = refs[:bands]
    solid_ref, next_ref = refs[bands : bands + 2]
    (held, elem, side, main, inv, res, dirn, image, sol, table, last_table, edge, solid, ends, sem) = refs[
        bands + 2 :
    ]
    sec, fx, fy = (lax.axis_index(axis) for axis in ("sec", "fx", "fy"))
    z_up = (sec & 1) == 0
    fields, cells_z, cells_y = air_ref.shape[:3]
    z_odds = [(m, parts[m]) for m in odd_masks(tiles_s)]
    across = sec ^ jnp.where(z_up, sec - 1, sec + 1)
    outer = [
        pltpu.make_async_copy(ends.at[i], next_ref.at[:, z], sem.at[2 + i])
        for i, z in enumerate((0, cells_z - 1))
    ]
    lane_tiles = [slice(i, i + LANES) for i in range(0, wide, LANES)]
    small = bands * wide <= SUBS * LANES

    def take(part, band):
        count = BAND_ROWS if small else SUBS

        def body(n, carry):
            for i, cut in enumerate(lane_tiles):
                held[i, pl.ds(band + n * (count * bands), count, stride=bands), :] = part[
                    pl.ds(n * count, count), cut
                ]
            return carry

        if small:
            body(0, 0)
        else:
            lax.fori_loop(0, BAND_ROWS // count, body, 0)

    @pl.when(fy >= 0)
    def _():
        for i, copy in enumerate(outer):
            for f in range(fields):
                span = slice(BAND_ROWS + f * cells_y, BAND_ROWS + (f + 1) * cells_y)
                even = parts[1][span, :LANES]
                odd = jnp.zeros_like(even)
                for m, part in z_odds:
                    odd = jnp.where(across == m, part[span, :LANES], odd)
                here, there = (odd, even) if i == 0 else (even, odd)
                ends[i, f] = ends_ref[i, f] + weight_ref[i] * jnp.where(z_up, here, there)
            copy.start()

    @pl.when(fy >= 0)
    def _():
        for j in range(tiles_y):
            for k in range(tiles_s):
                band = (sec ^ k) * tiles_y + (fy ^ j)
                take(parts[j * tiles_s + k], band)

    def loop(start, stop, body, carry):
        if not small:
            return lax.fori_loop(start, stop, body, carry)
        for h in range(start, stop):
            carry = body(h, carry)
        return carry

    def span_of(r):
        return pl.ds(r * bands if isinstance(r, int) else pl.multiple_of(r * bands, bands), bands)

    def join(tiles):
        return tiles[0] if len(tiles) == 1 else jnp.concatenate(tiles, axis=1)

    def row_of(ref, r):
        return join([ref[i, span_of(r), :] for i in range(len(lane_tiles))])

    def put(ref, r, x):
        for i, cut in enumerate(lane_tiles):
            ref[i, span_of(r), :] = x[:, cut]

    lane = iota((bands, wide), 1)
    band = iota((bands, wide), 0)
    used = lane < EW * tiles_x + 1

    def right(x):
        return pltpu.roll(x, wide - 1, 1)

    def left(x):
        return pltpu.roll(x, 1, 1)

    def plus(*terms):
        terms = [x for x in terms if x is not None]
        total = terms[0] if terms else None
        for x in terms[1:]:
            total = total + x
        return total

    def seam(low, high):
        below = jnp.where(band > 0, pltpu.roll(high, 1, 0), 0.0)
        above = jnp.where(band < bands - 1, pltpu.roll(low, bands - 1, 0), 0.0)
        return low + below, high + above

    def total_of(parts):
        x = plus(*parts)
        return jnp.sum(jnp.sum(x, axis=0, keepdims=True), axis=1, keepdims=True)

    def first_row(ref, x, n):
        return seam(x, row_of(ref, n + NH - 1))[0]

    def last_row(ref, x, n):
        return seam(row_of(ref, n - NH + 1), x)[1]

    def once(x):
        return jnp.where(band > 0, 0.0, x)

    zero = jnp.zeros((bands, wide), jnp.float32)

    @pl.when(fy >= 0)
    def _():
        def prepare(h, before):
            now = []
            for t in range(ET):
                kind = row_of(held, 2 * FIELD_ROWS + t * NH + h)
                x = jnp.zeros_like(kind)
                s = jnp.zeros_like(kind)
                for m in range(material_count):
                    x = jnp.where(kind == m + 1.0, conduct_ref[m] * (1.0 / 12.0), x)
                    s = jnp.where(kind == m + 1.0, capacity_ref[m] * 0.125, s)
                put(elem, t * NH + h, x)
                now += [x, 5.0 * x + s]
            both = [a + b for a, b in zip(now, before)]
            for t in range(NT):
                if t < ET:
                    x = both[2 * t]
                    put(side, t * NH + h, x + left(x))
                x = plus(both[2 * t + 1] if t < ET else None, both[2 * t - 1] if t else None)
                put(main, t * NH + h, x + left(x))
            return tuple(now)

        loop(0, NH, prepare, (zero,) * (2 * ET))

    def begin(h, acc, fix=None):
        out = []
        for t in range(NT):
            n = t * NH + h
            d, r = row_of(held, n), row_of(held, FIELD_ROWS + n)
            if fix is not None:
                d, r = fix(held, d, n), fix(held, r, FIELD_ROWS + n)
            v = jnp.where(used, 1.0 / d, 0.0)
            z = r * v
            put(inv, n, v)
            put(res, n, r)
            put(dirn, n, z)
            out.append(acc[t] + (once(r * z) if fix is first_row else r * z))
        return tuple(out)

    acc = begin(0, (zero,) * NT, first_row)
    acc = begin(NH - 1, acc, last_row)
    acc = loop(1, NH - 1, begin, acc)
    gamma = total_of(acc)

    def operate(iteration, beta, step_len):
        last = iteration + 1 == ITERS

        def fetch(h):
            p, y = [], []
            for t in range(NT):
                n = t * NH + h
                x = row_of(dirn, n)
                if beta is not None:
                    put(sol, n, plus(step_len * x, row_of(sol, n) if iteration > 1 else None))
                    x = row_of(res, n) * row_of(inv, n) + beta * x
                    put(dirn, n, x)
                p.append(x)
                y.append(right(x))
            return p, y

        def finish(h, p, diag_now, cross_now, on_diag, on_cross, acc):
            out_acc = []
            for t in range(NT):
                n = t * NH + h
                out = row_of(main, n) * p[t]
                if t < ET:
                    out = out + row_of(side, n) * p[t + 1]
                if t > 0:
                    out = out + row_of(side, n - NH) * p[t - 1]
                out = out - plus(
                    diag_now[t], on_cross[t], left(plus(cross_now[t], on_diag[t]))
                )
                if not last:
                    put(image, n, out)
                out_acc.append(acc[t] + p[t] * out)
            return out_acc

        def body(h, carry):
            p, y, on_diag, on_cross, acc = (carry[i * NT : (i + 1) * NT] for i in range(5))
            p_next, y_next = fetch(h + 1)
            diag = [p[t] + y_next[t] for t in range(NT)]
            cross = [y[t] + p_next[t] for t in range(NT)]
            layer = [a + b for a, b in zip(diag, cross)]
            x = [row_of(elem, t * NH + h) for t in range(ET)]
            diag_now, cross_now = [], []
            for t in range(NT):
                upper = x[t] if t < ET else None
                lower = x[t - 1] if t > 0 else None
                both = plus(upper, lower)
                other = plus(
                    upper * layer[t + 1] if t < ET else None,
                    lower * layer[t - 1] if t > 0 else None,
                )
                diag_now.append(other + both * diag[t])
                cross_now.append(other + both * cross[t])
            acc = finish(h, p, diag_now, cross_now, on_diag, on_cross, acc)
            return (*p_next, *y_next, *diag_now, *cross_now, *acc)

        p, y = fetch(0)
        carry = loop(0, EH, body, (*p, *y) + (zero,) * (3 * NT))
        p, y, on_diag, on_cross, acc = (carry[i * NT : (i + 1) * NT] for i in range(5))
        none = [None] * NT
        acc = finish(EH, p, none, none, on_diag, on_cross, acc)
        if last:
            for j in range(tiles_y):
                table[j] = pack(sol, j)
                last_table[j] = pack(dirn, j)
        return total_of(acc)

    spot = iota((NH, LANES), 1) >> 5

    def pack(ref, j):
        packed = None
        for t in range(NT):
            start = t * NH * bands + sec * tiles_y + j
            x = join(
                [ref[i, pl.ds(start, NH, stride=bands), :] for i in range(len(lane_tiles))]
            )
            x = pltpu.roll(x, (NW * t - EW * fx + tiles_x * wide) % wide, 1)[:, :LANES]
            packed = x if packed is None else jnp.where(spot == t, x, packed)
        return packed

    beta = step_len = None
    for iteration in range(ITERS):
        step_len = gamma / operate(iteration, beta, step_len)
        if iteration + 1 == ITERS:
            break

        def update(h, acc, fix=None, step_len=step_len):
            out = []
            for t in range(NT):
                n = t * NH + h
                q = row_of(image, n)
                if fix is not None:
                    q = fix(image, q, n)
                r = row_of(res, n) - step_len * q
                put(res, n, r)
                part = r * r * row_of(inv, n)
                out.append(acc[t] + (once(part) if fix is first_row else part))
            return tuple(out)

        acc = update(0, (zero,) * NT, first_row)
        acc = update(NH - 1, acc, last_row)
        gamma_next = total_of(loop(1, NH - 1, update, acc))
        beta = gamma_next / gamma
        gamma = gamma_next

    for j in range(tiles_y):
        table[j] = table[j] + step_len * last_table[j]
    last_table[0] = table[fy]
    first = pltpu.make_async_copy(solid, solid_ref, sem.at[0])
    second = pltpu.make_async_copy(edge, next_ref.at[0, :, 0:SUBS, :], sem.at[1])

    for copy in outer:
        copy.wait()

    @pl.when(fy == 0)
    def _():
        extra = look_up(
            lambda r: table[r // ROWS, r % ROWS : r % ROWS + 1], tiles_y * ROWS, wall_ref[...]
        )
        extra = extra * gain_ref[...]
        top = iota((SUBS, LANES), 0) == 0
        for z in range(cells_z):
            base = ends[z // (cells_z - 1), 0, :SUBS] if z in (0, cells_z - 1) else edge_ref[z]
            edge[z] = base + jnp.where(top, extra[z : z + 1], 0.0)
        second.start()

    @pl.when(fy >= 0)
    def _():
        solid[...] = look_up(lambda r: last_table[0, r : r + 1], ROWS, place_ref[...])
        first.start()

    @pl.when(fy == 0)
    def _():
        second.wait()

    first.wait()


def odd_masks(count):
    return sorted({i ^ (i + 1) for i in range(1, count - 1, 2)})


def swap(x, axis, mask):
    count = lax.axis_size(axis)
    return lax.ppermute(x, axis, [(i, i ^ mask) for i in range(count)])


def pair_swap(x, axis, odd):
    count = lax.axis_size(axis)
    pairs = []
    for i in range(odd, count - 1, 2):
        pairs += [(i, i + 1), (i + 1, i)]
    return lax.ppermute(x, axis, pairs) if pairs else jnp.zeros_like(x)


def on_device(
    conn,
    material,
    side_nodes,
    rim_nodes,
    iface_node,
    face_of_row,
    conductivity,
    capacity,
    diag_part,
    heat_source,
    air_state,
):
    f32 = jnp.float32
    tiles_s, tiles_x, tiles_y = (lax.axis_size(axis) for axis in ("sec", "fx", "fy"))
    bands = tiles_s * tiles_y
    wide = -(-(EW * tiles_x + 1) // LANES) * LANES
    fields, cells_z, cells_y, cells_x = air_state.shape

    def call(kernel, args, specs, outs, out_specs, scratch=(), **more):
        held = list(args) + list(outs) + [s for s in scratch if hasattr(s, "shape")]
        need = sum(4 * int(np.prod(x.shape)) for x in held)
        return pl.pallas_call(
            kernel,
            in_specs=specs,
            out_specs=out_specs,
            out_shape=outs,
            scratch_shapes=list(scratch),
            compiler_params=pltpu.CompilerParams(vmem_limit_bytes=need + (6 << 20)),
            **more,
        )(*args)

    def cost(microseconds):
        return pl.CostEstimate(
            flops=0, bytes_accessed=int(3.7e6 * microseconds), transcendentals=0
        )

    def shape(*dims):
        return jax.ShapeDtypeStruct(dims, f32)

    def ints(*dims):
        return jax.ShapeDtypeStruct(dims, jnp.int32)

    even, odd, nodes, air = call(
        stage_kernel,
        [
            pltpu.with_memory_space_constraint(x, pltpu.HBM)
            for x in (
                conn.reshape(conn.shape[-2:]),
                material.reshape(1, -1),
                diag_part.reshape(ROWS, LANES),
                heat_source.reshape(ROWS, LANES),
                air_state,
            )
        ],
        [HBM] * 5,
        [
            shape(3 * ROWS + cells_z, LANES),
            shape(3 * ROWS + cells_z, LANES),
            ints(ROWS, LANES),
            shape(*air_state.shape),
        ],
        [VMEM] * 4,
        [
            pltpu.VMEM(conn.shape[-2:], jnp.int32),
            pltpu.VMEM((1, material.shape[-1]), jnp.int32),
            pltpu.VMEM((ROWS, LANES), f32),
            pltpu.VMEM((ROWS, LANES), f32),
            pltpu.SemaphoreType.DMA((5,)),
        ],
    )
    odds = odd_masks(tiles_x)
    pays = [even] + [
        swap(odd if k in odds else even, "fx", k) for k in range(1, tiles_x)
    ]
    place, rows, y_even, y_odd, z_even, z_odd = call(
        place_kernel,
        [nodes, iface_node.reshape(1, -1), air],
        [VMEM] * 3,
        [ints(ROWS, LANES), shape(iface_node.shape[-1] // LANES, LANES)]
        + [shape(fields, cells_z, cells_x)] * 2
        + [shape(fields, cells_y, cells_x)] * 2,
        [VMEM] * 6,
        cost_estimate=cost(0.6),
    )

    y_ghosts = [pair_swap(y_even, "fy", 0)]
    if tiles_y > 2:
        y_ghosts.append(pair_swap(y_odd, "fy", 1))

    ghosts = list(y_ghosts)
    even, odd, both = call(
        lambda *refs: band_kernel(tiles_x, wide, *refs),
        pays + [rows, z_even, z_odd] + ghosts,
        [VMEM] * (tiles_x + 3) + [ANY] * len(ghosts),
        [shape(BAND_ROWS + fields * cells_y, wide)] * 2
        + [shape(BAND_ROWS + 2 * SUBS, wide)],
        [VMEM] * 3,
        [pltpu.VMEM((tiles_x, 3 * ROWS, LANES), f32)],
        cost_estimate=cost(0.3),
    )
    z_odds = odd_masks(tiles_s)
    own_bands = [even] + [
        swap(odd if k in z_odds else even, "sec", k) for k in range(1, tiles_s)
    ]
    boths = [both] + [swap(both, "fy", j) for j in range(1, tiles_y)]
    wall = call(
        lambda *refs: face_kernel(tiles_y, *refs),
        [face_of_row.reshape(-1, LANES)] + boths,
        [VMEM] * (1 + tiles_y),
        [ints(cells_z, LANES)],
        [VMEM],
        [pltpu.VMEM((tiles_y,) + rows.shape, f32)],
        cost_estimate=cost(0.5),
    )[0]

    ghosts += [pays[1]] + [pays[m] for m in odds]
    others = [wall] + [pays[k] for k in range(2, tiles_x) if k not in odds]
    air_next, edge, gain, ends, weight = call(
        lambda *refs: air_kernel(tiles_x, tiles_y, len(others), *refs),
        [air] + ghosts + others,
        [VMEM] * (1 + len(ghosts)) + [ANY] * len(others),
        [
            shape(*air_state.shape),
            shape(cells_z, SUBS, LANES),
            shape(cells_z, LANES),
            shape(2, fields, cells_y, cells_x),
            shape(2, cells_y, cells_x),
        ],
        [ANY] + [VMEM] * 4,
        [pltpu.VMEM((LANES, LANES), f32)] * 2
        + [pltpu.VMEM(air_state.shape, f32), pltpu.SemaphoreType.DMA],
        cost_estimate=cost(4.0),
    )

    marks = [edge, gain, ends]
    for k in range(1, tiles_s):
        i = (k - 1) % len(marks)
        own_bands[k], marks[i] = lax.optimization_barrier((own_bands[k], marks[i]))
    edge, gain, ends = marks
    all_bands = list(own_bands)
    for j in range(1, tiles_y):
        all_bands += [boths[j]] + [swap(b, "fy", j) for b in own_bands[1:]]

    grid = (wide // LANES, NT * NH * bands, LANES)
    solid, air_next = call(
        lambda *refs: solve_kernel(
            tiles_s, tiles_x, tiles_y, wide, conductivity.shape[0], *refs
        ),
        [conductivity, capacity, place, wall, edge, gain, ends, weight, air_next]
        + all_bands,
        [SMEM] * 2 + [VMEM] * 6 + [ANY] + [VMEM] * bands,
        [shape(ROWS, LANES), shape(*air_state.shape)],
        [ANY, ANY],
        [pltpu.VMEM((wide // LANES, BAND_ROWS * bands, LANES), f32)]
        + [pltpu.VMEM(grid, f32)] * 8
        + [
            pltpu.VMEM((tiles_y, ROWS, LANES), f32),
            pltpu.VMEM((tiles_y, ROWS, LANES), f32),
            pltpu.VMEM((cells_z, SUBS, LANES), f32),
            pltpu.VMEM((ROWS, LANES), f32),
            pltpu.VMEM((2, fields, cells_y, cells_x), f32),
            pltpu.SemaphoreType.DMA((4,)),
        ],
        input_output_aliases={8: 1},
    )
    return solid.reshape(diag_part.shape), air_next


def solution(mesh):
    return jax.shard_map(
        on_device,
        mesh=mesh,
        in_specs=(
            P("sec", "fx", "fy", None, None),
            P("sec", "fx", "fy", None),
            P("sec", "fx", "fy", None, None),
            P("sec", "fx", "fy", None, None),
            P("sec", "fx", "fy", None),
            P("sec", "fx", None),
            P(),
            P(),
            P("sec", "fx", "fy", None),
            P("sec", "fx", "fy", None),
            P(None, "sec", "fy", "fx"),
        ),
        out_specs=(P("sec", "fx", "fy", None), P(None, "sec", "fy", "fx")),
        check_vma=False,
    )
```

```python
import jax
import jax.numpy as jnp
import numpy as np
from jax import lax
from jax.experimental import pallas as pl
from jax.experimental.pallas import tpu as pltpu
from jax.sharding import PartitionSpec as P

NW = 32
NH = 24
NT = 4
ITERS = 4
LANES = 128
SUBS = 8

time_step = 0.2
viscosity = 0.75

VMEM = pl.BlockSpec(memory_space=pltpu.VMEM)
SMEM = pl.BlockSpec(memory_space=pltpu.SMEM)
ANY = pl.BlockSpec(memory_space=pl.ANY)
HBM = pl.BlockSpec(memory_space=pltpu.HBM)

EW = NW - 1
EH = NH - 1
ET = NT - 1
ELEMS = ET * EH * EW
ROWS = NT * NH * NW // LANES
FIELD_ROWS = NT * NH
BAND_ROWS = 2 * FIELD_ROWS + ET * NH


def iota(shape, dim):
    return lax.broadcasted_iota(jnp.int32, shape, dim)


def lane_pick(row, idx):
    return jnp.take_along_axis(
        jnp.broadcast_to(row, idx.shape), idx, axis=1, mode="promise_in_bounds"
    )


def look_up(load, count, place):
    outs = []
    for start in range(0, place.shape[0], SUBS):
        part = place[start : start + SUBS]
        high = part >> 7
        low = part & (LANES - 1)
        out = None
        for r in range(count):
            got = lane_pick(load(r), low)
            out = got if out is None else jnp.where(high == r, got, out)
        outs.append(out)
    return jnp.concatenate(outs, axis=0) if len(outs) > 1 else outs[0]


def spread(idx, values):
    count = idx.shape[0]
    acc = None
    group = 4
    for start in range(0, count, group):
        left, right = [], []
        for r in range(start, start + group):
            row = idx[r : r + 1]
            hot_high = iota((count, LANES), 0) == (row >> 7)
            hot_low = iota((LANES, LANES), 0) == (row & (LANES - 1))
            left.append(
                jnp.concatenate(
                    [jnp.where(hot_high, v[r : r + 1], 0.0) for v in values], axis=0
                ).astype(jnp.bfloat16)
            )
            right.append(jnp.where(hot_low, 1.0, 0.0).astype(jnp.bfloat16))
        part = lax.dot_general(
            jnp.concatenate(left, axis=1),
            jnp.concatenate(right, axis=1),
            (((1,), (1,)), ((), ())),
            preferred_element_type=jnp.float32,
        )
        acc = part if acc is None else acc + part
    return [acc[i * count : (i + 1) * count] for i in range(len(values))]


def element_keys():
    h = np.arange(NH)[:, None]
    lane = np.arange(LANES)[None, :]
    t, w = lane // NW, lane % NW
    corner = 4 * (t == NT - 1) + 2 * (h == NH - 1) + (w == NW - 1)
    column = np.minimum(t, ET - 1) * EH * EW + np.minimum(h, EH - 1) * EW + np.minimum(w, EW - 1)
    return corner, column


def stage_kernel(
    conn_hbm, material_hbm, diag_hbm, source_hbm, air_hbm,
    even_ref, odd_ref, nodes_ref, air_ref,
    conn_ref, material_ref, diag_ref, source_ref, sem,
):
    fx = lax.axis_index("fx")
    loads = [
        pltpu.make_async_copy(a, b, sem.at[i])
        for i, (a, b) in enumerate(
            [
                (conn_hbm, conn_ref),
                (diag_hbm, diag_ref),
                (source_hbm, source_ref),
                (material_hbm, material_ref),
                (air_hbm, air_ref),
            ]
        )
    ]
    for load in loads:
        load.start()
    corner_np, column_np = element_keys()
    last = ELEMS // LANES

    def column_tile(ref, c, k):
        start = ELEMS - LANES if k == last else LANES * k
        return ref[c : c + 1, start : start + LANES]

    loads[0].wait()
    loads[3].wait()
    pieces, kinds = [], []
    for j in range(NH // SUBS):
        h = iota((SUBS, LANES), 0) + SUBS * j
        lane = iota((SUBS, LANES), 1)
        t = lane >> 5
        w = lane & (NW - 1)
        corner = (
            jnp.where(t == NT - 1, 4, 0) + jnp.where(h == NH - 1, 2, 0) + jnp.where(w == NW - 1, 1, 0)
        )
        column = (
            jnp.minimum(t, ET - 1) * (EH * EW)
            + jnp.minimum(h, EH - 1) * EW
            + jnp.minimum(w, EW - 1)
        )
        tile = column >> 7
        low = jnp.where(tile == last, column - (ELEMS - LANES), column & (LANES - 1))
        key = tile * 8 + corner
        rows = slice(SUBS * j, SUBS * (j + 1))
        wanted = sorted(set((column_np[rows] // LANES * 8 + corner_np[rows]).reshape(-1).tolist()))
        out = jnp.zeros((SUBS, LANES), jnp.int32)
        for code in wanted:
            c, k = code % 8, code // 8
            out = jnp.where(key == code, lane_pick(column_tile(conn_ref, c, k), low), out)
        pieces.append(out)
        kind = jnp.full((SUBS, LANES), -1, jnp.int32)
        for k in sorted({code // 8 for code in wanted if code % 8 == 0}):
            row = column_tile(material_ref, 0, k)
            kind = jnp.where((corner == 0) & (tile == k), lane_pick(row, low), kind)
        kinds.append(kind)
    nodes = jnp.concatenate(pieces, axis=0)
    nodes_ref[...] = nodes
    loads[1].wait()
    loads[2].wait()
    diag = look_up(lambda r: diag_ref[r : r + 1], ROWS, nodes)
    source = look_up(lambda r: source_ref[r : r + 1], ROWS, nodes)
    kind = jnp.concatenate(kinds, axis=0).astype(jnp.float32) + 1.0
    for ref in (even_ref, odd_ref):
        ref[0:ROWS] = diag
        ref[ROWS : 2 * ROWS] = source
        ref[2 * ROWS : 3 * ROWS] = kind

    loads[4].wait()
    fields, cells_z, cells_y, cells_x = air_ref.shape
    x_up = (fx & 1) == 0
    lane = iota((cells_y, LANES), 1)
    lows, highs = [], []
    for f in range(fields):
        low = jnp.zeros((cells_y, LANES), jnp.float32)
        high = jnp.zeros((cells_y, LANES), jnp.float32)
        for z in range(cells_z):
            x = pltpu.roll(air_ref[f, z], z + 1, 1)
            high = jnp.where(lane == z, x, high)
            low = jnp.where(lane == z + 1, x, low)
        lows.append(low)
        highs.append(high)
    low = pltpu.roll(jnp.concatenate(lows, axis=0), LANES - 1, 1)
    high = jnp.concatenate(highs, axis=0)
    even_ref[3 * ROWS :] = jnp.where(x_up, high, low).T[:cells_z]
    odd_ref[3 * ROWS :] = jnp.where(x_up, low, high).T[:cells_z]


def band_kernel(tiles_x, wide, *refs):
    parts, (z_even, z_odd) = refs[:tiles_x], refs[tiles_x : tiles_x + 2]
    even_ref, odd_ref, held = refs[-3:]
    fields, cells_y = z_even.shape[:2]
    for f in range(fields):
        span = slice(BAND_ROWS + f * cells_y, BAND_ROWS + (f + 1) * cells_y)
        even_ref[span, :LANES] = z_even[f]
        odd_ref[span, :LANES] = z_odd[f]
    fx = lax.axis_index("fx")
    for k, part in enumerate(parts):
        held[fx ^ k] = part[0 : 3 * ROWS]
    lane = iota((NH, wide), 1)
    at = 0
    for field in range(3):
        for t in range(NT if field < 2 else ET):
            total = None
            for f in range(tiles_x):
                x = held[f, field * ROWS : (field + 1) * ROWS]
                if wide > LANES:
                    x = jnp.concatenate([x, jnp.zeros((NH, wide - LANES), jnp.float32)], axis=1)
                shift = (EW * f - NW * t) % wide
                if shift:
                    x = pltpu.roll(x, shift, 1)
                x = jnp.where((lane >= EW * f) & (lane < EW * f + NW), x, 0.0)
                total = x if total is None else total + x
            for ref in (even_ref, odd_ref):
                ref[at : at + NH] = total
            at += NH


def air_kernel(tiles_x, tiles_y, others, air_ref, *refs):
    refs = list(refs)
    y_even = refs.pop(0)
    y_odd = refs.pop(0) if tiles_y > 2 else None
    x_even = refs.pop(0)
    x_odds = [(m, refs.pop(0)) for m in odd_masks(tiles_x)]
    refs = refs[others:]
    next_hbm, edge_ref, gain_ref, ends_ref, weight_ref, west_ref, east_ref, next_ref, sem = refs
    fx, fy = lax.axis_index("fx"), lax.axis_index("fy")
    fields, cells_z, cells_y, cells_x = air_ref.shape
    x_up = (fx & 1) == 0
    y_up = (fy & 1) == 0
    even = x_even[3 * ROWS :]
    odd = jnp.zeros_like(even)
    partner = jnp.where(x_up, fx - 1, fx + 1)
    for m, ref in x_odds:
        odd = jnp.where((fx ^ partner) == m, ref[3 * ROWS :], odd)
    pad = jnp.zeros((LANES - cells_z, LANES), jnp.float32)
    west_ref[...] = jnp.concatenate([jnp.where(x_up, odd, even), pad], axis=0).T
    east_ref[...] = jnp.concatenate([jnp.where(x_up, even, odd), pad], axis=0).T
    row = iota((cells_y, LANES), 0)
    lane = iota((cells_y, LANES), 1)
    half = 0.5 * time_step
    mix = time_step * viscosity

    def layer(z, below, above):
        u, v, w = air_ref[1, z], air_ref[2, z], air_ref[3, z]
        hu, hv, hw = half * u, half * v, half * w
        gain_ref[pl.ds(z, 1), :] = (mix + hv[0:1]) * jnp.where(fy == 0, 1.0, 0.0)
        for f in range(fields):
            x = air_ref[f, z]
            span = slice(f * cells_y, (f + 1) * cells_y)
            west = jnp.where(
                lane == 0,
                pltpu.roll(west_ref[span], (LANES - z) % LANES, 1),
                pltpu.roll(x, 1, 1),
            )
            east = jnp.where(
                lane == LANES - 1,
                pltpu.roll(east_ref[span], LANES - 1 - z, 1),
                pltpu.roll(x, LANES - 1, 1),
            )
            y_e = y_even[f, pl.ds(z, 1), :]
            y_o = y_odd[f, pl.ds(z, 1), :] if y_odd is not None else jnp.zeros_like(y_e)
            south_ghost = jnp.where(y_up, y_o, y_e)
            north_ghost = jnp.where(y_up, y_e, y_o)
            south = jnp.where(row == 0, south_ghost, pltpu.roll(x, 1, 0))
            north = jnp.where(row == cells_y - 1, north_ghost, pltpu.roll(x, cells_y - 1, 0))
            lower, upper = below(f), above(f)
            out = (
                (1.0 - 6.0 * mix) * x
                + mix * (east + west + north + south + upper + lower)
                + hu * (west - east)
                + hv * (south - north)
                + hw * (lower - upper)
            )
            next_ref[f, z] = out
            if f == 0:
                edge_ref[z] = out[:SUBS]

    def outside(f):
        return jnp.zeros((cells_y, LANES), jnp.float32)

    steps = 4
    depth = cells_z // steps
    for step in range(steps):
        start, stop = step * depth, (step + 1) * depth
        if start == 0:
            layer(0, outside, lambda f: air_ref[f, 1])

        @pl.loop(max(start, 1), min(stop, cells_z - 1), unroll=True)
        def _(z):
            layer(z, lambda f: air_ref[f, z - 1], lambda f: air_ref[f, z + 1])

        if stop == cells_z:
            layer(cells_z - 1, lambda f: air_ref[f, cells_z - 2], outside)
        pltpu.make_async_copy(
            next_ref.at[:, start:stop], next_hbm.at[:, start:stop], sem
        ).start()
    for i, z in enumerate((0, cells_z - 1)):
        hw = half * air_ref[3, z]
        weight_ref[i] = mix - hw if i else mix + hw
        ends_ref[i] = next_ref[:, z]
    pltpu.make_async_copy(next_ref, next_hbm, sem).wait()


def place_kernel(
    nodes_ref, iface_ref, air_ref, place_ref, rows_ref, y_even, y_odd, z_even, z_odd
):
    sec, fy = lax.axis_index("sec"), lax.axis_index("fy")
    fields, cells_z, cells_y, cells_x = air_ref.shape
    z_up = (sec & 1) == 0
    z_even[...] = air_ref[:, jnp.where(z_up, cells_z - 1, 0)]
    z_odd[...] = air_ref[:, jnp.where(z_up, 0, cells_z - 1)]
    y_up = (fy & 1) == 0
    for f in range(fields):
        first = air_ref[f, :, 0, :]
        last = air_ref[f, :, cells_y - 1, :]
        y_even[f] = jnp.where(y_up, last, first)
        y_odd[f] = jnp.where(y_up, first, last)
    nodes = nodes_ref[...]
    at_row = iota(nodes.shape, 0).astype(jnp.float32)
    at_lane = iota(nodes.shape, 1).astype(jnp.float32)
    high, low = spread(nodes, [at_row, at_lane])
    place = high * LANES + low
    place_ref[...] = place.astype(jnp.int32)
    count = iface_ref.shape[-1] // LANES
    iface = jnp.concatenate(
        [iface_ref[0:1, LANES * r : LANES * (r + 1)] for r in range(count)], axis=0
    )
    rows_ref[...] = look_up(lambda r: place[r : r + 1], ROWS, iface)


def face_kernel(tiles_y, face_ref, *refs):
    parts, wall_ref, held = refs[:tiles_y], refs[tiles_y], refs[tiles_y + 1]
    fy = lax.axis_index("fy")
    for k, part in enumerate(parts):
        held[fy ^ k] = part[...] + (fy ^ k).astype(jnp.float32) * (ROWS * LANES)
    rows = jnp.concatenate([held[j] for j in range(tiles_y)], axis=0)
    row = rows.astype(jnp.int32)
    high, low = spread(
        face_ref[...],
        [(row >> 7).astype(jnp.float32), (row & (LANES - 1)).astype(jnp.float32)],
    )
    wall_ref[...] = (high * LANES + low).astype(jnp.int32)


def solve_kernel(
    tiles_s, tiles_x, tiles_y, wide, material_count,
    conduct_ref, capacity_ref, place_ref, wall_ref, edge_ref, gain_ref, ends_ref, weight_ref, air_ref,
    *refs,
):
    bands = tiles_s * tiles_y
    parts = refs[:bands]
    solid_ref, next_ref = refs[bands : bands + 2]
    (held, elem, side, main, inv, res, dirn, image, sol, table, last_table, edge, solid, ends, sem) = refs[
        bands + 2 :
    ]
    sec, fx, fy = (lax.axis_index(axis) for axis in ("sec", "fx", "fy"))
    z_up = (sec & 1) == 0
    fields, cells_z, cells_y = air_ref.shape[:3]
    z_odds = [(m, parts[m]) for m in odd_masks(tiles_s)]
    across = sec ^ jnp.where(z_up, sec - 1, sec + 1)
    outer = [
        pltpu.make_async_copy(ends.at[i], next_ref.at[:, z], sem.at[2 + i])
        for i, z in enumerate((0, cells_z - 1))
    ]
    lane_tiles = [slice(i, i + LANES) for i in range(0, wide, LANES)]
    small = bands * wide <= SUBS * LANES

    def take(part, band):
        count = BAND_ROWS if small else SUBS

        def body(n, carry):
            for i, cut in enumerate(lane_tiles):
                held[i, pl.ds(band + n * (count * bands), count, stride=bands), :] = part[
                    pl.ds(n * count, count), cut
                ]
            return carry

        if small:
            body(0, 0)
        else:
            lax.fori_loop(0, BAND_ROWS // count, body, 0)

    @pl.when(fy >= 0)
    def _():
        for i, copy in enumerate(outer):
            for f in range(fields):
                span = slice(BAND_ROWS + f * cells_y, BAND_ROWS + (f + 1) * cells_y)
                even = parts[1][span, :LANES]
                odd = jnp.zeros_like(even)
                for m, part in z_odds:
                    odd = jnp.where(across == m, part[span, :LANES], odd)
                here, there = (odd, even) if i == 0 else (even, odd)
                ends[i, f] = ends_ref[i, f] + weight_ref[i] * jnp.where(z_up, here, there)
            copy.start()

    @pl.when(fy >= 0)
    def _():
        for j in range(tiles_y):
            for k in range(tiles_s):
                band = (sec ^ k) * tiles_y + (fy ^ j)
                take(parts[j * tiles_s + k], band)

    def loop(start, stop, body, carry):
        if not small:
            return lax.fori_loop(start, stop, body, carry)
        for h in range(start, stop):
            carry = body(h, carry)
        return carry

    def span_of(r):
        return pl.ds(r * bands if isinstance(r, int) else pl.multiple_of(r * bands, bands), bands)

    def join(tiles):
        return tiles[0] if len(tiles) == 1 else jnp.concatenate(tiles, axis=1)

    def row_of(ref, r):
        return join([ref[i, span_of(r), :] for i in range(len(lane_tiles))])

    def put(ref, r, x):
        for i, cut in enumerate(lane_tiles):
            ref[i, span_of(r), :] = x[:, cut]

    lane = iota((bands, wide), 1)
    band = iota((bands, wide), 0)
    used = lane < EW * tiles_x + 1

    def right(x):
        return pltpu.roll(x, wide - 1, 1)

    def left(x):
        return pltpu.roll(x, 1, 1)

    def plus(*terms):
        terms = [x for x in terms if x is not None]
        total = terms[0] if terms else None
        for x in terms[1:]:
            total = total + x
        return total

    def seam(low, high):
        below = jnp.where(band > 0, pltpu.roll(high, 1, 0), 0.0)
        above = jnp.where(band < bands - 1, pltpu.roll(low, bands - 1, 0), 0.0)
        return low + below, high + above

    def total_of(parts):
        x = plus(*parts)
        return jnp.sum(jnp.sum(x, axis=0, keepdims=True), axis=1, keepdims=True)

    def first_row(ref, x, n):
        return seam(x, row_of(ref, n + NH - 1))[0]

    def last_row(ref, x, n):
        return seam(row_of(ref, n - NH + 1), x)[1]

    def once(x):
        return jnp.where(band > 0, 0.0, x)

    zero = jnp.zeros((bands, wide), jnp.float32)

    @pl.when(fy >= 0)
    def _():
        def prepare(h, before):
            now = []
            for t in range(ET):
                kind = row_of(held, 2 * FIELD_ROWS + t * NH + h)
                x = jnp.zeros_like(kind)
                s = jnp.zeros_like(kind)
                for m in range(material_count):
                    x = jnp.where(kind == m + 1.0, conduct_ref[m] * (1.0 / 12.0), x)
                    s = jnp.where(kind == m + 1.0, capacity_ref[m] * 0.125, s)
                put(elem, t * NH + h, x)
                now += [x, 5.0 * x + s]
            both = [a + b for a, b in zip(now, before)]
            for t in range(NT):
                if t < ET:
                    x = both[2 * t]
                    put(side, t * NH + h, x + left(x))
                x = plus(both[2 * t + 1] if t < ET else None, both[2 * t - 1] if t else None)
                put(main, t * NH + h, x + left(x))
            return tuple(now)

        loop(0, NH, prepare, (zero,) * (2 * ET))

    def begin(h, acc, fix=None):
        out = []
        for t in range(NT):
            n = t * NH + h
            d, r = row_of(held, n), row_of(held, FIELD_ROWS + n)
            if fix is not None:
                d, r = fix(held, d, n), fix(held, r, FIELD_ROWS + n)
            v = jnp.where(used, 1.0 / d, 0.0)
            z = r * v
            put(inv, n, v)
            put(res, n, r)
            put(dirn, n, z)
            out.append(acc[t] + (once(r * z) if fix is first_row else r * z))
        return tuple(out)

    acc = begin(0, (zero,) * NT, first_row)
    acc = begin(NH - 1, acc, last_row)
    acc = loop(1, NH - 1, begin, acc)
    gamma = total_of(acc)

    def operate(iteration, beta, step_len):
        last = iteration + 1 == ITERS

        def fetch(h):
            p, y = [], []
            for t in range(NT):
                n = t * NH + h
                x = row_of(dirn, n)
                if beta is not None:
                    put(sol, n, plus(step_len * x, row_of(sol, n) if iteration > 1 else None))
                    x = row_of(res, n) * row_of(inv, n) + beta * x
                    put(dirn, n, x)
                p.append(x)
                y.append(right(x))
            return p, y

        def finish(h, p, diag_now, cross_now, on_diag, on_cross, acc):
            out_acc = []
            for t in range(NT):
                n = t * NH + h
                out = row_of(main, n) * p[t]
                if t < ET:
                    out = out + row_of(side, n) * p[t + 1]
                if t > 0:
                    out = out + row_of(side, n - NH) * p[t - 1]
                out = out - plus(
                    diag_now[t], on_cross[t], left(plus(cross_now[t], on_diag[t]))
                )
                if not last:
                    put(image, n, out)
                out_acc.append(acc[t] + p[t] * out)
            return out_acc

        def body(h, carry):
            p, y, on_diag, on_cross, acc = (carry[i * NT : (i + 1) * NT] for i in range(5))
            p_next, y_next = fetch(h + 1)
            diag = [p[t] + y_next[t] for t in range(NT)]
            cross = [y[t] + p_next[t] for t in range(NT)]
            layer = [a + b for a, b in zip(diag, cross)]
            x = [row_of(elem, t * NH + h) for t in range(ET)]
            diag_now, cross_now = [], []
            for t in range(NT):
                upper = x[t] if t < ET else None
                lower = x[t - 1] if t > 0 else None
                both = plus(upper, lower)
                other = plus(
                    upper * layer[t + 1] if t < ET else None,
                    lower * layer[t - 1] if t > 0 else None,
                )
                diag_now.append(other + both * diag[t])
                cross_now.append(other + both * cross[t])
            acc = finish(h, p, diag_now, cross_now, on_diag, on_cross, acc)
            return (*p_next, *y_next, *diag_now, *cross_now, *acc)

        p, y = fetch(0)
        carry = loop(0, EH, body, (*p, *y) + (zero,) * (3 * NT))
        p, y, on_diag, on_cross, acc = (carry[i * NT : (i + 1) * NT] for i in range(5))
        none = [None] * NT
        acc = finish(EH, p, none, none, on_diag, on_cross, acc)
        if last:
            for j in range(tiles_y):
                table[j] = pack(sol, j)
                last_table[j] = pack(dirn, j)
        return total_of(acc)

    spot = iota((NH, LANES), 1) >> 5

    def pack(ref, j):
        packed = None
        for t in range(NT):
            start = t * NH * bands + sec * tiles_y + j
            x = join(
                [ref[i, pl.ds(start, NH, stride=bands), :] for i in range(len(lane_tiles))]
            )
            x = pltpu.roll(x, (NW * t - EW * fx + tiles_x * wide) % wide, 1)[:, :LANES]
            packed = x if packed is None else jnp.where(spot == t, x, packed)
        return packed

    beta = step_len = None
    for iteration in range(ITERS):
        step_len = gamma / operate(iteration, beta, step_len)
        if iteration + 1 == ITERS:
            break

        def update(h, acc, fix=None, step_len=step_len):
            out = []
            for t in range(NT):
                n = t * NH + h
                q = row_of(image, n)
                if fix is not None:
                    q = fix(image, q, n)
                r = row_of(res, n) - step_len * q
                put(res, n, r)
                part = r * r * row_of(inv, n)
                out.append(acc[t] + (once(part) if fix is first_row else part))
            return tuple(out)

        acc = update(0, (zero,) * NT, first_row)
        acc = update(NH - 1, acc, last_row)
        gamma_next = total_of(loop(1, NH - 1, update, acc))
        beta = gamma_next / gamma
        gamma = gamma_next

    for j in range(tiles_y):
        table[j] = table[j] + step_len * last_table[j]
    last_table[0] = table[fy]
    first = pltpu.make_async_copy(solid, solid_ref, sem.at[0])
    second = pltpu.make_async_copy(edge, next_ref.at[0, :, 0:SUBS, :], sem.at[1])

    for copy in outer:
        copy.wait()

    @pl.when(fy == 0)
    def _():
        extra = look_up(
            lambda r: table[r // ROWS, r % ROWS : r % ROWS + 1], tiles_y * ROWS, wall_ref[...]
        )
        extra = extra * gain_ref[...]
        top = iota((SUBS, LANES), 0) == 0
        for z in range(cells_z):
            base = ends[z // (cells_z - 1), 0, :SUBS] if z in (0, cells_z - 1) else edge_ref[z]
            edge[z] = base + jnp.where(top, extra[z : z + 1], 0.0)
        second.start()

    @pl.when(fy >= 0)
    def _():
        solid[...] = look_up(lambda r: last_table[0, r : r + 1], ROWS, place_ref[...])
        first.start()

    @pl.when(fy == 0)
    def _():
        second.wait()

    first.wait()


def odd_masks(count):
    return sorted({i ^ (i + 1) for i in range(1, count - 1, 2)})


def swap(x, axis, mask):
    count = lax.axis_size(axis)
    return lax.ppermute(x, axis, [(i, i ^ mask) for i in range(count)])


def pair_swap(x, axis, odd):
    count = lax.axis_size(axis)
    pairs = []
    for i in range(odd, count - 1, 2):
        pairs += [(i, i + 1), (i + 1, i)]
    return lax.ppermute(x, axis, pairs) if pairs else jnp.zeros_like(x)


def on_device(
    conn,
    material,
    side_nodes,
    rim_nodes,
    iface_node,
    face_of_row,
    conductivity,
    capacity,
    diag_part,
    heat_source,
    air_state,
):
    f32 = jnp.float32
    tiles_s, tiles_x, tiles_y = (lax.axis_size(axis) for axis in ("sec", "fx", "fy"))
    bands = tiles_s * tiles_y
    wide = -(-(EW * tiles_x + 1) // LANES) * LANES
    fields, cells_z, cells_y, cells_x = air_state.shape

    def call(kernel, args, specs, outs, out_specs, scratch=(), **more):
        held = list(args) + list(outs) + [s for s in scratch if hasattr(s, "shape")]
        need = sum(4 * int(np.prod(x.shape)) for x in held)
        return pl.pallas_call(
            kernel,
            in_specs=specs,
            out_specs=out_specs,
            out_shape=outs,
            scratch_shapes=list(scratch),
            compiler_params=pltpu.CompilerParams(vmem_limit_bytes=need + (6 << 20)),
            **more,
        )(*args)

    def cost(microseconds):
        return pl.CostEstimate(
            flops=0, bytes_accessed=int(3.7e6 * microseconds), transcendentals=0
        )

    def shape(*dims):
        return jax.ShapeDtypeStruct(dims, f32)

    def ints(*dims):
        return jax.ShapeDtypeStruct(dims, jnp.int32)

    even, odd, nodes, air = call(
        stage_kernel,
        [
            pltpu.with_memory_space_constraint(x, pltpu.HBM)
            for x in (
                conn.reshape(conn.shape[-2:]),
                material.reshape(1, -1),
                diag_part.reshape(ROWS, LANES),
                heat_source.reshape(ROWS, LANES),
                air_state,
            )
        ],
        [HBM] * 5,
        [
            shape(3 * ROWS + cells_z, LANES),
            shape(3 * ROWS + cells_z, LANES),
            ints(ROWS, LANES),
            shape(*air_state.shape),
        ],
        [VMEM] * 4,
        [
            pltpu.VMEM(conn.shape[-2:], jnp.int32),
            pltpu.VMEM((1, material.shape[-1]), jnp.int32),
            pltpu.VMEM((ROWS, LANES), f32),
            pltpu.VMEM((ROWS, LANES), f32),
            pltpu.SemaphoreType.DMA((5,)),
        ],
    )
    odds = odd_masks(tiles_x)
    pays = [even] + [
        swap(odd if k in odds else even, "fx", k) for k in range(1, tiles_x)
    ]
    place, rows, y_even, y_odd, z_even, z_odd = call(
        place_kernel,
        [nodes, iface_node.reshape(1, -1), air],
        [VMEM] * 3,
        [ints(ROWS, LANES), shape(iface_node.shape[-1] // LANES, LANES)]
        + [shape(fields, cells_z, cells_x)] * 2
        + [shape(fields, cells_y, cells_x)] * 2,
        [VMEM] * 6,
        cost_estimate=cost(0.6),
    )

    y_ghosts = [pair_swap(y_even, "fy", 0)]
    if tiles_y > 2:
        y_ghosts.append(pair_swap(y_odd, "fy", 1))

    wall = call(
        lambda *refs: face_kernel(tiles_y, *refs),
        [face_of_row.reshape(-1, LANES), rows] + [swap(rows, "fy", j) for j in range(1, tiles_y)],
        [VMEM] * (1 + tiles_y),
        [ints(cells_z, LANES)],
        [VMEM],
        [pltpu.VMEM((tiles_y,) + rows.shape, f32)],
        cost_estimate=cost(0.5),
    )[0]
    ghosts = list(y_ghosts)
    even, odd = call(
        lambda *refs: band_kernel(tiles_x, wide, *refs),
        pays + [z_even, z_odd, wall] + ghosts,
        [VMEM] * (tiles_x + 2) + [ANY] * (1 + len(ghosts)),
        [shape(BAND_ROWS + fields * cells_y, wide)] * 2,
        [VMEM] * 2,
        [pltpu.VMEM((tiles_x, 3 * ROWS, LANES), f32)],
        cost_estimate=cost(0.3),
    )
    z_odds = odd_masks(tiles_s)
    own_bands = [even] + [
        swap(odd if k in z_odds else even, "sec", k) for k in range(1, tiles_s)
    ]
    ghosts += [pays[1]] + [pays[m] for m in odds]
    others = [pays[k] for k in range(2, tiles_x) if k not in odds]
    air_next, edge, gain, ends, weight = call(
        lambda *refs: air_kernel(tiles_x, tiles_y, len(others), *refs),
        [air] + ghosts + others,
        [VMEM] * (1 + len(ghosts)) + [ANY] * len(others),
        [
            shape(*air_state.shape),
            shape(cells_z, SUBS, LANES),
            shape(cells_z, LANES),
            shape(2, fields, cells_y, cells_x),
            shape(2, cells_y, cells_x),
        ],
        [ANY] + [VMEM] * 4,
        [pltpu.VMEM((LANES, LANES), f32)] * 2
        + [pltpu.VMEM(air_state.shape, f32), pltpu.SemaphoreType.DMA],
        cost_estimate=cost(4.0),
    )

    marks = [edge, gain, ends]
    for k in range(1, tiles_s):
        i = (k - 1) % len(marks)
        own_bands[k], marks[i] = lax.optimization_barrier((own_bands[k], marks[i]))
    edge, gain, ends = marks
    all_bands = list(own_bands)
    for j in range(1, tiles_y):
        all_bands += [swap(b, "fy", j) for b in own_bands]

    grid = (wide // LANES, NT * NH * bands, LANES)
    solid, air_next = call(
        lambda *refs: solve_kernel(
            tiles_s, tiles_x, tiles_y, wide, conductivity.shape[0], *refs
        ),
        [conductivity, capacity, place, wall, edge, gain, ends, weight, air_next]
        + all_bands,
        [SMEM] * 2 + [VMEM] * 6 + [ANY] + [VMEM] * bands,
        [shape(ROWS, LANES), shape(*air_state.shape)],
        [ANY, ANY],
        [pltpu.VMEM((wide // LANES, BAND_ROWS * bands, LANES), f32)]
        + [pltpu.VMEM(grid, f32)] * 8
        + [
            pltpu.VMEM((tiles_y, ROWS, LANES), f32),
            pltpu.VMEM((tiles_y, ROWS, LANES), f32),
            pltpu.VMEM((cells_z, SUBS, LANES), f32),
            pltpu.VMEM((ROWS, LANES), f32),
            pltpu.VMEM((2, fields, cells_y, cells_x), f32),
            pltpu.SemaphoreType.DMA((4,)),
        ],
        input_output_aliases={8: 1},
    )
    return solid.reshape(diag_part.shape), air_next


def solution(mesh):
    return jax.shard_map(
        on_device,
        mesh=mesh,
        in_specs=(
            P("sec", "fx", "fy", None, None),
            P("sec", "fx", "fy", None),
            P("sec", "fx", "fy", None, None),
            P("sec", "fx", "fy", None, None),
            P("sec", "fx", "fy", None),
            P("sec", "fx", None),
            P(),
            P(),
            P("sec", "fx", "fy", None),
            P("sec", "fx", "fy", None),
            P(None, "sec", "fy", "fx"),
        ),
        out_specs=(P("sec", "fx", "fy", None), P(None, "sec", "fy", "fx")),
        check_vma=False,
    )
```
